32 devices in a mesh: dp: 8 (over z, x), cls: 4 (over y, core).
Axes of the slice: x: 2, y: 2, z: 4, core: 2. Of those that a mesh axis runs over, the one named last changes fastest.
Arguments:
- images: bfloat16 [4096, 128, 128], P('dp'), may hold values from -6 to 6
- references: bfloat16 [2304, 8192], P(('dp', 'cls')), may hold values from -0.0625 to 0.0625
- best_class: int32 [4096, 4], P('dp'), may hold values from 0 to 63, as said below
- best_rot: int32 [4096, 4], P('dp'), may hold values from 0 to 35
- prior: float32 [4096, 4], P('dp'), may hold values from 0.1 to 1
- precision: float32 [4096], P('dp'), may hold values from 0.5 to 200
Outputs:
- class_sums: float32 [2304, 8192], P(('dp', 'cls'))
The draws below stay inside these ranges and needn't reach their ends.
Inputs may be any that keep to these rules, and one draw needn't show every extreme that they name: In each aligned block of 512 particles, the panels best_class * 36 + best_rot of at most 128 of the block's pairs lie among the 72 panels of one holder (panel // 72); one holder reaches exactly 128 in every block.
All inputs are finite; a program needn't handle non-finite values.
Results may differ from the reference program's by a relative error of at most 0.012.
The reference program's roundings to bfloat16 on the way count: a program that leaves them out, or rounds other values in their place, can miss the bound.
Values may be sent and summed in bfloat16 or wider, within the bound.
No kernel may reach another device: no remote copies, remote signals or barrier semaphores. Data moves between devices by JAX's collectives and lax.ppermute only.
A program may use at most 192 MiB of HBM per device.

```python
import math
import jax
import jax.numpy as jnp
from jax import lax

BOX = 128
KWIN = 64
ROTS = 36
TOP = 4
P_DEV = 512
FEAT = 8192
PANELS = 2304
PART = 4096
OWNERS = 32
PAN_DEV = 72
PAIR = 2048
CAP = 128
N_DP = 8


def pose_table(key):
    base_key = jax.random.fold_in(key, 11)
    heavy_key, block_key = jax.random.split(base_key)
    heavy_owner = jax.random.randint(heavy_key, (), 0, OWNERS).astype(jnp.int32)

    def one_block(bkey):
        perm_key, shuffle_key, panel_key = jax.random.split(bkey, 3)
        chosen = jax.random.permutation(perm_key, (OWNERS - 1) * CAP)[:PAIR - CAP].astype(jnp.int32)
        marks = jnp.zeros(((OWNERS - 1) * CAP,), jnp.int32).at[chosen].set(1).reshape(OWNERS - 1, CAP)
        slot_rank = (jnp.cumsum(marks, axis=1) - 1).reshape((OWNERS - 1) * CAP).astype(jnp.int32)
        light_owner = (chosen // CAP).astype(jnp.int32)
        light_owner = light_owner + (light_owner >= heavy_owner).astype(jnp.int32)
        light_rank = slot_rank[chosen]
        owner_ids = jnp.concatenate([jnp.full((CAP,), heavy_owner, jnp.int32), light_owner.astype(jnp.int32)])
        rank_ids = jnp.concatenate([jnp.arange(CAP, dtype=jnp.int32), light_rank.astype(jnp.int32)])
        offset_table = jax.vmap(lambda okey: jax.random.permutation(okey, PAN_DEV).astype(jnp.int32))(jax.random.split(panel_key, OWNERS))
        offsets = offset_table[owner_ids, rank_ids % PAN_DEV].astype(jnp.int32)
        panel_ids = (owner_ids * PAN_DEV + offsets).astype(jnp.int32)
        order = jax.random.permutation(shuffle_key, PAIR).astype(jnp.int32)
        return panel_ids[order].astype(jnp.int32)
    panel_ids = jax.vmap(one_block)(jax.random.split(block_key, N_DP))
    return panel_ids.reshape(PART, TOP).astype(jnp.int32)


def draw_best_class(key, part):
    panel_ids = pose_table(key)
    return (panel_ids // ROTS).astype(jnp.int32)


def draw_best_rot(key, part):
    panel_ids = pose_table(key)
    return (panel_ids % ROTS).astype(jnp.int32)


def draw_precision(key, part):
    key = jax.random.fold_in(key, 5)
    upper = 4.0
    logs = jax.random.uniform(key, (PART,), jnp.float32, jnp.log(0.5), jnp.log(upper))
    return jnp.exp(logs).astype(jnp.float32)


def block_scale(stream_key, dims, cuts, smallest, top_value):
    level = 1.0
    for axis_at, shards_of in cuts:
        draws = jax.random.uniform(jax.random.fold_in(jax.random.fold_in(stream_key, 6), axis_at), (shards_of,), jnp.float32, smallest / len(cuts), top_value / len(cuts))
        level = level * jnp.repeat(jnp.exp(draws), dims[axis_at] // shards_of).reshape((-1,) + (1,) * (len(dims) - 1 - axis_at))
    return level


def bell_draw(stream_key, shape, scale, limit, pieces=(), kind=jnp.bfloat16):
    result = jax.random.normal(stream_key, shape, jnp.float32) * scale
    if len(pieces) > 0:
        result = block_scale(stream_key, shape, pieces, -0.22, 0.18) * result
    return jnp.clip(result, min=-limit, max=limit).astype(kind)


def setup_inputs(seed: int = 0) -> dict:
    arg_keys = jax.random.split(jax.random.key(seed), 7)
    return {
        "images": bell_draw(arg_keys[0], (PART, BOX, BOX), 1.0, 6.0, ((0, 8),)),
        "references": bell_draw(arg_keys[1], (PANELS, FEAT), FEAT ** -0.5, 0.0625, ((0, 32),)),
        "best_class": draw_best_class(jax.random.fold_in(arg_keys[6], 71), 0),
        "best_rot": draw_best_rot(jax.random.fold_in(arg_keys[6], 71), 0),
        "prior": jnp.clip(jnp.exp(math.log(1.0) - 2.3025851 * jax.random.uniform(arg_keys[4], (PART, TOP), jnp.float32) ** block_scale(arg_keys[4], (PART, TOP), ((0, 8),), -0.2, 0.2)), 0.1, 1.0),
        "precision": draw_precision(jax.random.fold_in(arg_keys[6], 71), 0),
    }


def transform_tables(box_size, kwin_size):
    positions = jnp.arange(box_size, dtype=jnp.float32)
    frequencies = jnp.arange(kwin_size, dtype=jnp.float32) - float(kwin_size // 2)
    phase_x = 2.0 * math.pi * positions[:, None] * frequencies[None, :] / box_size
    x_table = (jnp.concatenate([jnp.cos(phase_x), -jnp.sin(phase_x)], axis=1) / box_size).astype(jnp.bfloat16)
    angle_y = 2.0 * math.pi * frequencies[:, None] * positions[None, :] / box_size
    cosine = jnp.cos(angle_y)
    sine_part = jnp.sin(angle_y)
    real_rows = jnp.stack([cosine, sine_part], axis=1)
    imag_rows = jnp.stack([-sine_part, cosine], axis=1)
    y_table = jnp.stack([real_rows, imag_rows], axis=0).astype(jnp.bfloat16)
    return x_table, y_table


def to_spectra(image_block, x_table, y_table):
    particle_count = image_block.shape[0]
    box_size = image_block.shape[1]
    flat_images = image_block.reshape(particle_count * box_size, box_size)
    half_transform = jnp.dot(flat_images, x_table, preferred_element_type=jnp.float32).astype(jnp.bfloat16)
    half_transform = half_transform.reshape(particle_count, box_size, 2, KWIN)
    spectrum = jnp.einsum("pyck,oqcy->pkoq", half_transform.astype(jnp.float32), y_table.astype(jnp.float32))
    return spectrum.reshape(particle_count, FEAT).astype(jnp.bfloat16)


def reference(images, references, best_class, best_rot, prior, precision):
    x_table, y_table = transform_tables(BOX, KWIN)
    panel_ids = (best_class * ROTS + best_rot).astype(jnp.int32)
    blocks = PART // P_DEV
    block_inputs = (images.reshape(blocks, P_DEV, BOX, BOX), panel_ids.reshape(blocks, P_DEV, TOP),
                    prior.reshape(blocks, P_DEV, TOP), precision.reshape(blocks, P_DEV))
    panels_t = references.T

    def accumulate(class_sums, block_data):
        image_block, block_panels, prior_block, precision_block = block_data
        spectrum = to_spectra(image_block, x_table, y_table)
        raw_scores = jnp.dot(spectrum, panels_t, preferred_element_type=jnp.float32)
        picked = jnp.take_along_axis(raw_scores, block_panels, axis=1) * precision_block[:, None]
        peak_value = jnp.max(picked, axis=1, keepdims=True)
        unscaled = prior_block * jnp.exp(picked - peak_value)
        weights_bf = (unscaled / jnp.sum(unscaled, axis=1, keepdims=True)).astype(jnp.bfloat16)
        weighted = weights_bf.astype(jnp.float32)[:, :, None] * spectrum.astype(jnp.float32)[:, None, :]
        weighted = weighted.reshape(P_DEV * TOP, FEAT)
        class_sums = class_sums + jax.ops.segment_sum(weighted, block_panels.reshape(P_DEV * TOP), num_segments=PANELS)
        return class_sums, None

    start_sums = jnp.zeros((PANELS, FEAT), jnp.float32)
    class_sums, unused = lax.scan(accumulate, start_sums, block_inputs)
    return class_sums
```

```python
import functools
import math

import numpy as np
import jax
import jax.numpy as jnp
from jax import lax
from jax.experimental import pallas as pl
from jax.experimental.pallas import tpu as pltpu
from jax.sharding import PartitionSpec as P

KWIN = 64
HALF = KWIN // 2
ROTS = 36
TOP = 4
LANES = 2 * KWIN
UNIQUE = (HALF + 1) * LANES
ROW_PAD = 72
VMEM_BYTES = 24 * 1024 * 1024
CUT = 17


def half_tables(box):
    positions = np.arange(box, dtype=np.float32)
    frequencies = np.arange(KWIN, dtype=np.float32) - float(HALF)
    phase_x = (2.0 * math.pi * positions[:, None] * frequencies[None, : HALF + 1] / box).astype(np.float32)
    x_rows = np.zeros((ROW_PAD, box), np.float32)
    x_rows[: HALF + 1] = np.cos(phase_x).T / box
    x_rows[HALF + 1 : 2 * HALF + 2] = -np.sin(phase_x).T / box
    angle = (2.0 * math.pi * positions[:, None] * frequencies[None, :] / box).astype(np.float32)
    cosine, sine = np.cos(angle), np.sin(angle)
    y_rows = np.zeros((2 * box, 2 * LANES), np.float32)
    y_rows[:box, :KWIN] = cosine
    y_rows[:box, KWIN:LANES] = -sine
    y_rows[box:, :KWIN] = sine
    y_rows[box:, KWIN:LANES] = cosine
    y_rows[:box, LANES : LANES + KWIN] = cosine[:, :1]
    y_rows[:box, LANES + KWIN :] = -sine[:, :1]
    y_rows[box:, LANES : LANES + KWIN] = -sine[:, :1]
    y_rows[box:, LANES + KWIN :] = -cosine[:, :1]
    return jnp.asarray(x_rows, jnp.bfloat16), jnp.asarray(y_rows, jnp.bfloat16)


def mirror_matrix():
    m = np.zeros((LANES, LANES), np.float32)
    for q in range(1, KWIN):
        m[KWIN - q, q] = 1.0
        m[LANES - q, KWIN + q] = -1.0
    return jnp.asarray(m, jnp.bfloat16)


def lane_q(shape):
    return lax.broadcasted_iota(jnp.int32, shape, 1) % KWIN


def full_spec(shape):
    return pl.BlockSpec(shape, lambda *_: (0,) * len(shape))


def params(**kw):
    return pltpu.CompilerParams(vmem_limit_bytes=VMEM_BYTES, **kw)


def group(k):
    return slice(k * LANES, (k + 1) * LANES)


def fold_kernel(r_ref, m_ref, *outs):
    rows = r_ref.shape[0]
    q = lane_q((rows, LANES))
    mirror = m_ref[...]
    flip = lambda v: jnp.dot(v, mirror, preferred_element_type=jnp.float32)

    def put(k, value):
        for out_ref, first, last in zip(outs, (0, CUT), (CUT, HALF + 1)):
            if first <= k < last:
                out_ref[:, group(k - first)] = value.astype(out_ref.dtype)

    put(0, r_ref[:, group(0)])
    centre = r_ref[:, group(HALF)]
    special = centre.astype(jnp.float32)
    special = special + jnp.where((q >= 1) & (q < HALF), flip(centre), 0.0)
    for k in range(1, HALF):
        other = r_ref[:, group(KWIN - k)]
        put(k, r_ref[:, group(k)].astype(jnp.float32) + flip(other))
        edge = pltpu.roll(other.astype(jnp.float32), KWIN - k, 1)
        special = jnp.where(q == KWIN - k, edge, special)
    put(HALF, special)


def widths():
    return CUT * LANES, UNIQUE - CUT * LANES


def fold(references, mirror):
    rows = references.shape[0]
    return pl.pallas_call(
        fold_kernel,
        out_shape=[jax.ShapeDtypeStruct((rows, w), jnp.bfloat16) for w in widths()],
        compiler_params=params(),
        name="fold",
    )(references, mirror)


def unfold_kernel(m_ref, *rest):
    terms, out_ref = rest[:-1], rest[-1]
    rows = out_ref.shape[0]
    q = lane_q((rows, LANES))
    mirror = m_ref[...]
    count = len(terms) // 2

    def total(k):
        chosen, at = (terms[:count], k) if k < CUT else (terms[count:], k - CUT)
        return sum(t[:, group(at)].astype(jnp.float32) for t in chosen)

    def flip(v):
        high = v.astype(jnp.bfloat16)
        low = (v - high.astype(jnp.float32)).astype(jnp.bfloat16)
        return jnp.dot(high, mirror, preferred_element_type=jnp.float32) + jnp.dot(
            low, mirror, preferred_element_type=jnp.float32
        )

    special = total(HALF)
    out_ref[:, group(0)] = total(0)
    out_ref[:, group(HALF)] = jnp.where(q <= HALF, special, flip(special))
    for k in range(1, HALF):
        value = total(k)
        out_ref[:, group(k)] = value
        edge = pltpu.roll(special, LANES - (KWIN - k), 1)
        out_ref[:, group(KWIN - k)] = jnp.where(q == 0, edge, flip(value))


def unfold(left, right, mirror):
    terms = list(left) + list(right)
    rows = terms[0].shape[0]
    return pl.pallas_call(
        unfold_kernel,
        out_shape=jax.ShapeDtypeStruct((rows, KWIN * LANES), jnp.float32),
        compiler_params=params(),
        name="unfold",
    )(mirror, *terms)


def dft_kernel(img_ref, x_ref, y_ref, *rest):
    out_ref, rows_scratch, lhs_scratch = rest[-3:]
    tile, box, _ = img_ref.shape
    x_rows = x_ref[...]
    step = 8
    for start in range(0, tile, step):
        pixels = img_ref[start : start + step].reshape(step * box, box)
        h = lax.dot_general(
            x_rows, pixels, (((1,), (1,)), ((), ())), preferred_element_type=jnp.float32
        )
        for i in range(step):
            at = (start + i) * ROW_PAD
            rows_scratch[at : at + ROW_PAD, :] = h[:, i * box : (i + 1) * box]
    for k in range(HALF + 1):
        for c in range(2):
            j = c * (HALF + 1) + k
            picked = rows_scratch[pl.ds(j, tile, stride=ROW_PAD), :]
            lhs_scratch[k * tile : (k + 1) * tile, c * box : (c + 1) * box] = picked.astype(jnp.bfloat16)
    y_rows = y_ref[...]
    q = lane_q((tile, LANES))
    special = jnp.zeros((tile, LANES), jnp.float32)
    batch = 11
    for k in range(HALF + 1):
        if k % batch == 0:
            many = jnp.dot(
                lhs_scratch[k * tile : (k + batch) * tile, :], y_rows, preferred_element_type=jnp.float32
            )
        both = many[(k % batch) * tile : (k % batch + 1) * tile]
        value = both[:, :LANES]
        if k < HALF:
            out_ref[:, group(k)] = value.astype(jnp.bfloat16)
        else:
            special = jnp.where(q <= HALF, value, special)
        if 0 < k < HALF:
            special = jnp.where(q == KWIN - k, both[:, LANES:], special)
    out_ref[:, group(HALF)] = special.astype(jnp.bfloat16)


def dft(images, x_rows, y_rows, tile, part=0, parts=1, earlier=None):
    count, box, _ = images.shape
    steps = count // (tile * parts)
    first = part * steps
    operands = [images, x_rows, y_rows]
    in_specs = [
        pl.BlockSpec((tile, box, box), lambda i: (first + i, 0, 0)),
        full_spec(x_rows.shape),
        full_spec(y_rows.shape),
    ]
    aliases = {}
    if earlier is not None:
        operands.append(earlier)
        in_specs.append(pl.BlockSpec(memory_space=pl.ANY))
        aliases = {3: 0}
    return pl.pallas_call(
        dft_kernel,
        grid=(steps,),
        in_specs=in_specs,
        out_specs=pl.BlockSpec((tile, UNIQUE), lambda i: (first + i, 0)),
        out_shape=jax.ShapeDtypeStruct((count, UNIQUE), jnp.bfloat16),
        scratch_shapes=[
            pltpu.VMEM((tile * ROW_PAD, box), jnp.float32),
            pltpu.VMEM(((HALF + 1) * tile, 2 * box), jnp.bfloat16),
        ],
        input_output_aliases=aliases,
        cost_estimate=pl.CostEstimate(
            flops=count // parts * (2 * box * box * ROW_PAD + 2 * (HALF + 1) * 2 * box * LANES * 2),
            bytes_accessed=2 * count // parts * (box * box + UNIQUE),
            transcendentals=0,
        ),
        compiler_params=params(),
        name="dft",
    )(*operands)


def stacked_rows(at, base_ref, rows, particles):
    parts = [
        lax.broadcasted_iota(jnp.int32, (rows, particles), 0) + base_ref[n] for n in at
    ]
    return jnp.concatenate(parts, axis=0) if len(parts) > 1 else parts[0]


def score_kernel(at, first, base_ref, spec_ref, panel_ref, before_ref, *rest):
    refs, out_ref = rest[:-1], rest[-1]
    particles = spec_ref.shape[0]
    rows, width = refs[0].shape
    block = refs[0][...] if len(refs) == 1 else jnp.concatenate([r[...] for r in refs], axis=0)
    s = lax.dot_general(
        block,
        spec_ref[:, first : first + width],
        (((1,), (1,)), ((), ())),
        preferred_element_type=jnp.float32,
    )
    row = stacked_rows(at, base_ref, rows, particles)
    for t in range(TOP):
        hit = row == panel_ref[t : t + 1, :]
        picked = jnp.sum(jnp.where(hit, s, 0.0), axis=0, keepdims=True)
        out_ref[t : t + 1, :] = before_ref[t : t + 1, :] + picked


def score(bases, at, piece, spectrum, panel, before, refs):
    rows, width = refs[0].shape
    particles = spectrum.shape[0]
    return pl.pallas_call(
        functools.partial(score_kernel, at, piece * CUT * LANES),
        in_specs=[pl.BlockSpec(memory_space=pltpu.SMEM)]
        + [pl.BlockSpec(memory_space=pltpu.VMEM)] * (3 + len(refs)),
        out_shape=jax.ShapeDtypeStruct(panel.shape, jnp.float32),
        cost_estimate=pl.CostEstimate(
            flops=2 * len(refs) * rows * particles * width * 2,
            bytes_accessed=2 * width * (particles + rows * len(refs)),
            transcendentals=0,
        ),
        compiler_params=params(),
        name="score",
    )(bases, spectrum, panel, before, *refs)


def weight_kernel(scores_ref, prior_ref, precision_ref, out_ref):
    value = jnp.sum(scores_ref[...], axis=0) * precision_ref[...]
    unscaled = prior_ref[...] * jnp.exp(value - jnp.max(value, axis=0, keepdims=True))
    weight = unscaled / jnp.sum(unscaled, axis=0, keepdims=True)
    out_ref[...] = weight.astype(jnp.bfloat16).astype(jnp.float32)


def weights_of(scores, prior, precision):
    return pl.pallas_call(
        weight_kernel,
        out_shape=jax.ShapeDtypeStruct(prior.shape, jnp.float32),
        compiler_params=params(),
        name="weights",
    )(scores, prior, precision)


def sums_kernel(at, first, base_ref, weight_ref, panel_ref, spec_ref, *outs):
    particles = spec_ref.shape[0]
    rows, width = outs[0].shape
    row = stacked_rows(at, base_ref, rows, particles)
    select = jnp.zeros(row.shape, jnp.float32)
    for t in range(TOP):
        select = select + jnp.where(row == panel_ref[t : t + 1, :], weight_ref[t : t + 1, :], 0.0)
    total = jnp.dot(
        select.astype(jnp.bfloat16),
        spec_ref[:, first : first + width],
        preferred_element_type=jnp.float32,
    )
    for n, out_ref in enumerate(outs):
        out_ref[...] = total[n * rows : (n + 1) * rows].astype(out_ref.dtype)


def sums(bases, at, piece, dtypes, weight, panel, spectrum, rows):
    particles = spectrum.shape[0]
    width = widths()[piece]
    return pl.pallas_call(
        functools.partial(sums_kernel, at, piece * CUT * LANES),
        in_specs=[pl.BlockSpec(memory_space=pltpu.SMEM)] + [pl.BlockSpec(memory_space=pltpu.VMEM)] * 3,
        out_shape=[jax.ShapeDtypeStruct((rows, width), d) for d in dtypes],
        cost_estimate=pl.CostEstimate(
            flops=2 * len(dtypes) * rows * particles * width * 2,
            bytes_accessed=2 * width * (particles + rows * len(dtypes)),
            transcendentals=0,
        ),
        compiler_params=params(),
        name="sums",
    )(bases, weight, panel, spectrum)


LINE = 4
GATHER_ORDER = ((0, 1, 2, 3), (1, 0, 1, 2), (2, 2, 3, 1), (3, 3, 0, 0))
SCATTER_ORDER = ((3, 0, 3, 0), (2, 3, 0, 1), (1, 2, 1, 2), (0, 1, 2, 3))


def block_places():
    table = np.zeros((2 * LINE, 16), np.int32)
    for place in range(2 * LINE):
        z, x = divmod(place, 2)
        gather = [order[z] for order in GATHER_ORDER]
        scatter = [order[z] for order in SCATTER_ORDER]
        table[place] = (
            [2 * g + x for g in gather]
            + [2 * g + 1 - x for g in gather]
            + [2 * g + x for g in scatter]
            + [2 * g + 1 - x for g in scatter]
        )
    return table


def along_z(hops):
    return [(2 * a + x, 2 * b + x) for a, b in hops for x in range(2)]


def move(value, hops):
    return lax.ppermute(value, "dp", along_z(hops))


def swap_x(value):
    return lax.ppermute(value, "dp", [(d, d ^ 1) for d in range(2 * LINE)])


def sum_of(terms):
    return functools.reduce(lambda a, b: a + b, terms)


def tie(*values):
    return lax.optimization_barrier(values)


def by_line(images, references, panel, prior, precision):
    rows = references.shape[0]
    cls_count = lax.axis_size("cls")
    mine = lax.axis_index("cls")
    place = lax.axis_index("dp")
    z = lax.shift_right_logical(place, 1)
    x_rows, y_rows = half_tables(images.shape[1])
    mirror = mirror_matrix()
    bases = (jnp.asarray(block_places())[place] * cls_count + mine) * rows
    here, there, keep, give = (range(4 * n, 4 * n + 4) for n in range(4))

    pieces = range(2)
    blocks = [[] for _ in pieces]
    own = fold(references, mirror)
    steps = []
    for p in pieces:
        u1 = move(own[p], ((0, 1), (1, 2), (2, 3)))
        d1 = move(own[p], ((1, 0), (2, 1), (3, 2)))
        steps.append((u1, d1, swap_x(own[p])))
    spectrum = dft(images, x_rows, y_rows, 64, 0, 2)
    (u1, d1, x1), (v1, w1, y1) = steps
    u1, d1, x1, spectrum = tie(u1, d1, x1, spectrum)
    v1, w1, y1 = tie(v1, w1, y1)
    steps = [(u1, d1, x1), (v1, w1, y1)]

    later = []
    for p in pieces:
        u1, d1, x1 = steps[p]
        u2 = move(u1, ((1, 2), (2, 3)))
        d2 = move(d1, ((1, 0), (2, 1)))
        s1 = jnp.where(z == 0, d1, u1)
        later.append([u2, d2, swap_x(s1)])
        blocks[p] += [own[p], x1, s1]
    spectrum = dft(images, x_rows, y_rows, 64, 1, 2, spectrum)
    *later[0], spectrum = tie(*later[0], spectrum)
    later[1] = tie(*later[1])

    last = []
    for p in pieces:
        u1, d1, x1 = steps[p]
        u2, d2, x2 = later[p]
        inner = jnp.where(z == 1, d2, u2)
        e3 = move(inner, ((2, 3), (1, 0)))
        s2 = jnp.where(z == 0, d2, jnp.where(z == 3, u2, d1))
        last.append([inner, e3, swap_x(s2)])
        blocks[p] += [x2, s2]
    order = (here[0], there[0], here[1], there[1], here[2])
    picked = jnp.zeros(panel.shape, jnp.float32)
    picked = score(bases, order, 0, spectrum, panel, picked, blocks[0])
    _, last[0][1], last[0][2], picked = tie(last[0][0], last[0][1], last[0][2], picked)
    picked = score(bases, order, 1, spectrum, panel, picked, blocks[1])
    last[1][1:] = tie(*last[1][1:])

    ends = []
    for p in pieces:
        inner, e3, x3 = last[p]
        s3 = jnp.where((z == 1) | (z == 2), inner, e3)
        ends.append(swap_x(s3))
        picked = score(bases, (there[2], here[3]), p, spectrum, panel, picked, [x3, s3])
    for p in pieces:
        picked = score(bases, (there[3],), p, spectrum, panel, picked, [ends[p]])

    scores = lax.all_gather(picked, "cls", axis=0, tiled=False)
    weight = weights_of(scores, prior, precision)

    narrow, wide = jnp.bfloat16, jnp.float32
    add = lambda *terms: sum_of([t.astype(wide) for t in terms]).astype(narrow)
    part = functools.partial(sums, bases, weight=weight, panel=panel, spectrum=spectrum, rows=rows)

    first = []
    for p in pieces:
        (g1,) = part((give[0],), p, [narrow])
        first.append(swap_x(g1))
    second = []
    for p in pieces:
        k1, g2 = part((keep[0], give[1]), p, [wide, narrow])
        r1, g2 = tie(first[p], g2)
        q1 = add(k1, r1)
        e2 = move(q1, ((0, 1), (3, 2)))
        second.append((q1, e2, swap_x(g2)))
    third = []
    for p in pieces:
        q1, e2, r2 = second[p]
        k2, g3 = part((keep[1], give[2]), p, [wide, narrow])
        e2, r2, g3 = tie(e2, r2, g3)
        q2 = add(k2, r2, e2)
        u3 = move(q2, ((0, 1), (1, 2)))
        d3 = move(q2, ((2, 1), (3, 2)))
        third.append((q1, u3, d3, swap_x(g3)))
    halves = []
    for p in pieces:
        q1, u3, d3, r3 = third[p]
        k3, g4 = part((keep[2], give[3]), p, [wide, narrow])
        u3, d3, r3, g4 = tie(u3, d3, r3, g4)
        q3 = add(k3, r3)
        up = add(jnp.where(z == 2, q1, q3), u3)
        down = add(jnp.where(z == 1, q1, q3), d3)
        u4 = move(up, ((0, 1), (1, 2), (2, 3)))
        d4 = move(down, ((1, 0), (2, 1), (3, 2)))
        r4 = swap_x(g4)
        (k4,) = part((keep[3],), p, [wide])
        halves.append([k4, r4, u4, d4])
    return unfold(halves[0], halves[1], mirror)


def by_collectives(images, references, panel, prior, precision):
    rows = references.shape[0]
    dp_count = lax.axis_size("dp")
    cls_count = lax.axis_size("cls")
    mine = lax.axis_index("cls")
    x_rows, y_rows = half_tables(images.shape[1])
    mirror = mirror_matrix()
    spectrum = dft(images, x_rows, y_rows, 64)
    bases = (jnp.arange(dp_count, dtype=jnp.int32) * cls_count + mine) * rows
    picked = jnp.zeros(panel.shape, jnp.float32)
    for p, own in enumerate(fold(references, mirror)):
        gathered = lax.all_gather(own, "dp", axis=0, tiled=False)
        for n in range(dp_count):
            picked = score(bases, (n,), p, spectrum, panel, picked, [gathered[n]])
    scores = lax.all_gather(picked, "cls", axis=0, tiled=False)
    weight = weights_of(scores, prior, precision)
    halves = []
    for p in range(2):
        partial = [
            sums(bases, (n,), p, [jnp.bfloat16], weight, panel, spectrum, rows)[0] for n in range(dp_count)
        ]
        halves.append([lax.psum_scatter(jnp.stack(partial), "dp", scatter_dimension=0, tiled=False)])
    return unfold(halves[0], halves[1], mirror)


def on_device(images, references, best_class, best_rot, prior, precision):
    panel = (best_class * ROTS + best_rot).T
    plan = by_line if lax.axis_size("dp") == 2 * LINE else by_collectives
    return plan(images, references, panel, prior.T, precision[None, :])


def solution(mesh):
    in_specs = (
        P("dp", None, None),
        P(("dp", "cls"), None),
        P("dp", None),
        P("dp", None),
        P("dp", None),
        P("dp"),
    )
    out_specs = P(("dp", "cls"), None)
    return jax.shard_map(on_device, mesh=mesh, in_specs=in_specs, out_specs=out_specs, check_vma=False)
```

```python
import functools
import math

import numpy as np
import jax
import jax.numpy as jnp
from jax import lax
from jax.experimental import pallas as pl
from jax.experimental.pallas import tpu as pltpu
from jax.sharding import PartitionSpec as P

KWIN = 64
HALF = KWIN // 2
ROTS = 36
TOP = 4
LANES = 2 * KWIN
UNIQUE = (HALF + 1) * LANES
ROW_PAD = 72
CUT = 17
WIDTHS = (CUT * LANES, UNIQUE - CUT * LANES)


def half_tables(box):
    positions = np.arange(box, dtype=np.float32)
    frequencies = np.arange(KWIN, dtype=np.float32) - float(HALF)
    phase_x = (2.0 * math.pi * positions[:, None] * frequencies[None, : HALF + 1] / box).astype(np.float32)
    x_rows = np.zeros((ROW_PAD, box), np.float32)
    x_rows[: HALF + 1] = np.cos(phase_x).T / box
    x_rows[HALF + 1 : 2 * HALF + 2] = -np.sin(phase_x).T / box
    angle = (2.0 * math.pi * positions[:, None] * frequencies[None, :] / box).astype(np.float32)
    cosine, sine = np.cos(angle), np.sin(angle)
    y_rows = np.zeros((2 * box, 2 * LANES), np.float32)
    y_rows[:box, :KWIN] = cosine
    y_rows[:box, KWIN:LANES] = -sine
    y_rows[box:, :KWIN] = sine
    y_rows[box:, KWIN:LANES] = cosine
    y_rows[:box, LANES : LANES + KWIN] = cosine[:, :1]
    y_rows[:box, LANES + KWIN :] = -sine[:, :1]
    y_rows[box:, LANES : LANES + KWIN] = -sine[:, :1]
    y_rows[box:, LANES + KWIN :] = -cosine[:, :1]
    x_wide = np.concatenate([x_rows, np.zeros((ROW_PAD, 2 * LANES - box), np.float32)], axis=1)
    return jnp.asarray(np.concatenate([y_rows, x_wide]), jnp.bfloat16)


def mirror_matrix():
    row = lax.broadcasted_iota(jnp.int32, (LANES, LANES), 0)
    col = lax.broadcasted_iota(jnp.int32, (LANES, LANES), 1)
    value = jnp.where(col < KWIN, 1.0, -1.0)
    hit = (row % KWIN + col % KWIN == KWIN) & (row // KWIN == col // KWIN)
    return jnp.where(hit, value, 0.0).astype(jnp.bfloat16)


def lane_q(shape):
    return lax.broadcasted_iota(jnp.int32, shape, 1) % KWIN


def full_spec(shape):
    return pl.BlockSpec(shape, lambda *_: (0,) * len(shape))


def params(megabytes=24):
    return pltpu.CompilerParams(vmem_limit_bytes=megabytes * 1024 * 1024)


def group(k):
    return slice(k * LANES, (k + 1) * LANES)


def fold_kernel(r_ref, *outs):
    rows = r_ref.shape[0]
    q = lane_q((rows, LANES))
    mirror = mirror_matrix()
    flip = lambda v: jnp.dot(v, mirror, preferred_element_type=jnp.float32)

    def put(k, value):
        out_ref, at = (outs[0], k) if k < CUT else (outs[1], k - CUT)
        out_ref[:, group(at)] = value.astype(out_ref.dtype)

    put(0, r_ref[:, group(0)])
    centre = r_ref[:, group(HALF)]
    special = centre.astype(jnp.float32)
    special = special + jnp.where((q >= 1) & (q < HALF), flip(centre), 0.0)
    for k in range(1, HALF):
        other = r_ref[:, group(KWIN - k)]
        put(k, r_ref[:, group(k)].astype(jnp.float32) + flip(other))
        edge = pltpu.roll(other.astype(jnp.float32), KWIN - k, 1)
        special = jnp.where(q == KWIN - k, edge, special)
    put(HALF, special)


def fold(references):
    rows = references.shape[0]
    return pl.pallas_call(
        fold_kernel,
        out_shape=[jax.ShapeDtypeStruct((rows, width), jnp.bfloat16) for width in WIDTHS],
        compiler_params=params(),
        name="fold",
    )(references)


def unfold_kernel(*rest):
    terms, out_ref = rest[:-1], rest[-1]
    rows = out_ref.shape[0]
    q = lane_q((rows, LANES))
    mirror = mirror_matrix()
    count = len(terms) // 2

    def total(k):
        chosen, at = (terms[:count], k) if k < CUT else (terms[count:], k - CUT)
        return sum(t[:, group(at)].astype(jnp.float32) for t in chosen)

    def flip(v):
        high = v.astype(jnp.bfloat16)
        low = (v - high.astype(jnp.float32)).astype(jnp.bfloat16)
        return jnp.dot(high, mirror, preferred_element_type=jnp.float32) + jnp.dot(
            low, mirror, preferred_element_type=jnp.float32
        )

    special = total(HALF)
    out_ref[:, group(0)] = total(0)
    out_ref[:, group(HALF)] = jnp.where(q <= HALF, special, flip(special))
    for k in range(1, HALF):
        value = total(k)
        out_ref[:, group(k)] = value
        edge = pltpu.roll(special, LANES - (KWIN - k), 1)
        out_ref[:, group(KWIN - k)] = jnp.where(q == 0, edge, flip(value))


def unfold(left, right):
    terms = list(left) + list(right)
    rows = terms[0].shape[0]
    return pl.pallas_call(
        unfold_kernel,
        out_shape=jax.ShapeDtypeStruct((rows, KWIN * LANES), jnp.float32),
        compiler_params=params(),
        name="unfold",
    )(*terms)


def dft_kernel(tile, first, table_ref, img_ref, out_ref, pixel_scratch, rows_scratch, lhs_scratch, sems):
    count, box = out_ref.shape[0], img_ref.shape[1]
    tiles = count // tile

    def copy(n):
        return pltpu.make_async_copy(
            img_ref.at[pl.ds(first + n * tile, tile)], pixel_scratch.at[n], sems.at[n]
        )

    for n in range(tiles):
        copy(n).start()
    y_rows = table_ref[: 2 * box, :]
    x_rows = table_ref[2 * box :, :box]
    q = lane_q((tile, LANES))
    step, batch = 8, 11

    def one(n, carry):
        copy(n).wait()
        for start in range(0, tile, step):
            pixels = pixel_scratch[n, start : start + step].reshape(step * box, box)
            h = lax.dot_general(
                x_rows, pixels, (((1,), (1,)), ((), ())), preferred_element_type=jnp.float32
            )
            for i in range(step):
                at = (start + i) * ROW_PAD
                rows_scratch[at : at + ROW_PAD, :] = h[:, i * box : (i + 1) * box]
        for k in range(HALF + 1):
            for c in range(2):
                j = c * (HALF + 1) + k
                picked = rows_scratch[pl.ds(j, tile, stride=ROW_PAD), :]
                lhs_scratch[k * tile : (k + 1) * tile, c * box : (c + 1) * box] = picked.astype(jnp.bfloat16)
        here = pl.ds(pl.multiple_of(n * tile, tile), tile)
        special = jnp.zeros((tile, LANES), jnp.float32)
        for k in range(HALF + 1):
            if k % batch == 0:
                many = jnp.dot(
                    lhs_scratch[k * tile : (k + batch) * tile, :], y_rows, preferred_element_type=jnp.float32
                )
            both = many[(k % batch) * tile : (k % batch + 1) * tile]
            value = both[:, :LANES]
            if k < HALF:
                out_ref[here, group(k)] = value.astype(jnp.bfloat16)
            else:
                special = jnp.where(q <= HALF, value, special)
            if 0 < k < HALF:
                special = jnp.where(q == KWIN - k, both[:, LANES:], special)
        out_ref[here, group(HALF)] = special.astype(jnp.bfloat16)
        return carry

    lax.fori_loop(0, tiles, one, 0)


def dft(images, table, tile, part, parts):
    count, box = images.shape[0] // parts, images.shape[1]
    return pl.pallas_call(
        functools.partial(dft_kernel, tile, part * count),
        in_specs=[pl.BlockSpec(memory_space=pltpu.VMEM), pl.BlockSpec(memory_space=pl.ANY)],
        out_shape=jax.ShapeDtypeStruct((count, UNIQUE), jnp.bfloat16),
        scratch_shapes=[
            pltpu.VMEM((count // tile, tile, box, box), jnp.bfloat16),
            pltpu.VMEM((tile * ROW_PAD, box), jnp.float32),
            pltpu.VMEM(((HALF + 1) * tile, 2 * box), jnp.bfloat16),
            pltpu.SemaphoreType.DMA((count // tile,)),
        ],
        cost_estimate=pl.CostEstimate(
            flops=count * (2 * box * box * ROW_PAD + 2 * (HALF + 1) * 2 * box * LANES * 2),
            bytes_accessed=2 * count * (box * box + UNIQUE),
            transcendentals=0,
        ),
        compiler_params=params(46),
        name="dft",
    )(table, images)


def stacked_rows(at, base_ref, rows, particles):
    parts = [
        lax.broadcasted_iota(jnp.int32, (rows, particles), 0) + base_ref[n] for n in at
    ]
    return jnp.concatenate(parts, axis=0) if len(parts) > 1 else parts[0]


def stacked_rows(at, base_ref, rows, particles):
    parts = [
        lax.broadcasted_iota(jnp.int32, (rows, particles), 0) + base_ref[n] for n in at
    ]
    return jnp.concatenate(parts, axis=0) if len(parts) > 1 else parts[0]


def score_kernel(items, halves, base_ref, panel_ref, before_ref, *rest):
    specs, refs, out_ref = rest[:halves], list(rest[halves:-1]), rest[-1]
    rows = refs[0].shape[0]
    taken = []
    for at, first, width in items:
        blocks = [refs.pop(0)[...] for _ in at]
        taken.append((at, first, width, jnp.concatenate(blocks, axis=0) if len(blocks) > 1 else blocks[0]))
    edge = 0
    for spec_ref in specs:
        particles = spec_ref.shape[0]
        lanes = slice(edge, edge + particles)
        edge += particles
        picked = [before_ref[t : t + 1, lanes] for t in range(TOP)]
        for at, first, width, block in taken:
            s = lax.dot_general(
                block,
                spec_ref[:, first : first + width],
                (((1,), (1,)), ((), ())),
                preferred_element_type=jnp.float32,
            )
            row = stacked_rows(at, base_ref, rows, particles)
            for t in range(TOP):
                hit = row == panel_ref[t : t + 1, lanes]
                picked[t] = picked[t] + jnp.sum(jnp.where(hit, s, 0.0), axis=0, keepdims=True)
        for t in range(TOP):
            out_ref[t : t + 1, lanes] = picked[t]


def score(bases, spectra, panel, before, items):
    rows = items[0][2][0].shape[0]
    refs = [r for _, _, blocks in items for r in blocks]
    values = sum(r.shape[1] for r in refs) * rows
    shapes = [(at, first, blocks[0].shape[1]) for at, first, blocks in items]
    return pl.pallas_call(
        functools.partial(score_kernel, shapes, len(spectra)),
        in_specs=[pl.BlockSpec(memory_space=pltpu.SMEM)]
        + [pl.BlockSpec(memory_space=pltpu.VMEM)] * (2 + len(spectra) + len(refs)),
        out_shape=jax.ShapeDtypeStruct(panel.shape, jnp.float32),
        cost_estimate=pl.CostEstimate(
            flops=2 * values * panel.shape[1], bytes_accessed=2 * values, transcendentals=0
        ),
        compiler_params=params(),
        name="score",
    )(bases, panel, before, *spectra, *refs)


def weight_kernel(scores_ref, prior_ref, precision_ref, out_ref):
    value = jnp.sum(scores_ref[...], axis=0) * precision_ref[...]
    unscaled = prior_ref[...] * jnp.exp(value - jnp.max(value, axis=0, keepdims=True))
    weight = unscaled / jnp.sum(unscaled, axis=0, keepdims=True)
    out_ref[...] = weight.astype(jnp.bfloat16).astype(jnp.float32)


def weights_of(scores, prior, precision):
    return pl.pallas_call(
        weight_kernel,
        out_shape=jax.ShapeDtypeStruct(prior.shape, jnp.float32),
        compiler_params=params(),
        name="weights",
    )(scores, prior, precision)


def sums_kernel(items, halves, base_ref, weight_ref, panel_ref, *rest):
    specs, outs = rest[:halves], list(rest[halves:])
    particles = panel_ref.shape[1]
    for at, first in items:
        rows, width = outs[0].shape
        row = stacked_rows(at, base_ref, rows, particles)
        select = jnp.zeros(row.shape, jnp.float32)
        for t in range(TOP):
            select = select + jnp.where(row == panel_ref[t : t + 1, :], weight_ref[t : t + 1, :], 0.0)
        select = select.astype(jnp.bfloat16)
        total, edge = None, 0
        for spec_ref in specs:
            count = spec_ref.shape[0]
            term = jnp.dot(
                select[:, edge : edge + count],
                spec_ref[:, first : first + width],
                preferred_element_type=jnp.float32,
            )
            total = term if total is None else total + term
            edge += count
        for n in range(len(at)):
            out_ref = outs.pop(0)
            out_ref[...] = total[n * rows : (n + 1) * rows].astype(out_ref.dtype)


def sums(bases, weight, panel, spectra, rows, items, dtype):
    particles = panel.shape[1]
    shapes = [(rows, width) for at, _, width in items for _ in at]
    values = sum(a * b for a, b in shapes)
    return pl.pallas_call(
        functools.partial(sums_kernel, [(at, first) for at, first, _ in items], len(spectra)),
        in_specs=[pl.BlockSpec(memory_space=pltpu.SMEM)]
        + [pl.BlockSpec(memory_space=pltpu.VMEM)] * (2 + len(spectra)),
        out_shape=[jax.ShapeDtypeStruct(shape, dtype) for shape in shapes],
        cost_estimate=pl.CostEstimate(
            flops=2 * values * particles, bytes_accessed=4 * values, transcendentals=0
        ),
        compiler_params=params(),
        name="sums",
    )(bases, weight, panel, *spectra)


RING = (0, 2, 4, 6, 7, 5, 3, 1)


def ring_places():
    count = len(RING)
    table = np.zeros((count, count), np.int32)
    for at, place in enumerate(RING):
        table[place] = [RING[(at + d) % count] for d in range(count)]
    return table


def onward(value):
    return lax.ppermute(value, "dp", list(zip(RING, RING[1:] + RING[:1])))


def backward(value):
    return lax.ppermute(value, "dp", list(zip(RING[1:] + RING[:1], RING)))


def tie(*values):
    return lax.optimization_barrier(values)


def by_ring(images, references, panel, prior, precision):
    rows = references.shape[0]
    cls_count = lax.axis_size("cls")
    place, mine = lax.axis_index("dp"), lax.axis_index("cls")
    table = half_tables(images.shape[1])
    bases = (jnp.asarray(ring_places())[place] * cls_count + mine) * rows
    starts = (0, WIDTHS[0])

    own = fold(references)
    p1 = onward(own[0]), backward(own[1])
    q1 = onward(own[1]), backward(own[0])
    left = dft(images, table, 64, 0, 2)
    *p1, left, table = tie(*p1, left, table)
    p2 = onward(p1[0]), backward(p1[1])
    *q1, table = tie(*q1, table)
    q2 = onward(q1[0]), backward(q1[1])
    right = dft(images, table, 64, 1, 2)
    *p2, right = tie(*p2, right)
    p3 = onward(p2[0]), backward(p2[1])
    *q2, right = tie(*q2, right)
    q3 = onward(q2[0]), backward(q2[1])
    spectra = [left, right]
    picked = jnp.zeros(panel.shape, jnp.float32)
    near = [
        ((0, 7, 1), starts[0], [own[0], p1[0], q1[1]]),
        ((0, 7, 1), starts[1], [own[1], q1[0], p1[1]]),
        ((6, 2), starts[0], [p2[0], q2[1]]),
        ((6, 2), starts[1], [q2[0], p2[1]]),
    ]
    picked = score(bases, spectra, panel, picked, near)
    *p3, picked = tie(*p3, picked)
    p4 = onward(p3[0]), backward(p3[1])
    *q3, picked = tie(*q3, picked)
    middle = [((5, 3), starts[0], [p3[0], q3[1]]), ((5, 3), starts[1], [q3[0], p3[1]])]
    picked = score(bases, spectra, panel, picked, middle)
    *p4, picked = tie(*p4, picked)
    picked = score(bases, spectra, panel, picked, [((4,), starts[p], [p4[p]]) for p in range(2)])

    scores = lax.all_gather(picked, "cls", axis=0, tiled=False)
    weight = weights_of(scores, prior, precision)

    narrow, wide = jnp.bfloat16, jnp.float32
    part = functools.partial(sums, bases, weight, panel, spectra, rows)
    pieces = [(starts[p], WIDTHS[p]) for p in range(2)]
    far0, back0, far1, ahead1 = part([((4, 5), *pieces[0]), ((4, 3), *pieces[1])], narrow)
    p = onward(far0), backward(far1)
    q = onward(ahead1), backward(back0)
    rest = part([((3, 2, 6, 1, 7, 0), *pieces[0]), ((5, 2, 6, 1, 7, 0), *pieces[1])], wide)

    def pass_on(arrived, held):
        onto = [(h + a.astype(wide)).astype(narrow) for h, a in zip(held, arrived)]
        return onward(onto[0]), backward(onto[1])

    p = tie(*p)
    p = pass_on(p, (rest[0], rest[6]))
    q = pass_on(q, (rest[7], rest[2]))
    p = pass_on(p, (rest[1], rest[8]))
    q = pass_on(q, (rest[9], rest[4]))
    p = pass_on(p, (rest[3], rest[10]))
    return unfold([rest[5], p[0], q[1]], [rest[11], q[0], p[1]])


def by_collectives(images, references, panel, prior, precision):
    rows = references.shape[0]
    dp_count = lax.axis_size("dp")
    cls_count = lax.axis_size("cls")
    mine = lax.axis_index("cls")
    table = half_tables(images.shape[1])
    own = jnp.concatenate(fold(references), axis=1)
    gathered = lax.all_gather(own, "dp", axis=0, tiled=False)
    spectra = [dft(images, table, 64, part, 2) for part in range(2)]
    bases = (jnp.arange(dp_count, dtype=jnp.int32) * cls_count + mine) * rows
    picked = jnp.zeros(panel.shape, jnp.float32)
    items = [((n,), 0, [gathered[n]]) for n in range(dp_count)]
    for start in range(0, dp_count, 8):
        picked = score(bases, spectra, panel, picked, items[start : start + 8])
    scores = lax.all_gather(picked, "cls", axis=0, tiled=False)
    weight = weights_of(scores, prior, precision)
    partial = []
    for start in range(0, dp_count, 8):
        items = [((n,), 0, UNIQUE) for n in range(start, min(start + 8, dp_count))]
        partial += sums(bases, weight, panel, spectra, rows, items, jnp.bfloat16)
    half = lax.psum_scatter(jnp.stack(partial), "dp", scatter_dimension=0, tiled=False)
    return unfold([half[:, : WIDTHS[0]]], [half[:, WIDTHS[0] :]])


def on_device(images, references, best_class, best_rot, prior, precision):
    panel = (best_class * ROTS + best_rot).T
    plan = by_ring if lax.axis_size("dp") == len(RING) else by_collectives
    return plan(images, references, panel, prior.T, precision[None, :])


def solution(mesh):
    in_specs = (
        P("dp", None, None),
        P(("dp", "cls"), None),
        P("dp", None),
        P("dp", None),
        P("dp", None),
        P("dp"),
    )
    out_specs = P(("dp", "cls"), None)
    return jax.shard_map(on_device, mesh=mesh, in_specs=in_specs, out_specs=out_specs, check_vma=False)
```

```python
import functools
import math

import numpy as np
import jax
import jax.numpy as jnp
from jax import lax
from jax.experimental import pallas as pl
from jax.experimental.pallas import tpu as pltpu
from jax.sharding import PartitionSpec as P

KWIN = 64
HALF = KWIN // 2
ROTS = 36
TOP = 4
LANES = 2 * KWIN
UNIQUE = (HALF + 1) * LANES
ROW_PAD = 72
CUT = 17
WIDTHS = (CUT * LANES, UNIQUE - CUT * LANES)


def half_tables(box):
    positions = np.arange(box, dtype=np.float32)
    frequencies = np.arange(KWIN, dtype=np.float32) - float(HALF)
    phase_x = (2.0 * math.pi * positions[:, None] * frequencies[None, : HALF + 1] / box).astype(np.float32)
    x_rows = np.zeros((ROW_PAD, box), np.float32)
    x_rows[: HALF + 1] = np.cos(phase_x).T / box
    x_rows[HALF + 1 : 2 * HALF + 2] = -np.sin(phase_x).T / box
    angle = (2.0 * math.pi * positions[:, None] * frequencies[None, :] / box).astype(np.float32)
    cosine, sine = np.cos(angle), np.sin(angle)
    y_rows = np.zeros((2 * box, 2 * LANES), np.float32)
    y_rows[:box, :KWIN] = cosine
    y_rows[:box, KWIN:LANES] = -sine
    y_rows[box:, :KWIN] = sine
    y_rows[box:, KWIN:LANES] = cosine
    y_rows[:box, LANES : LANES + KWIN] = cosine[:, :1]
    y_rows[:box, LANES + KWIN :] = -sine[:, :1]
    y_rows[box:, LANES : LANES + KWIN] = -sine[:, :1]
    y_rows[box:, LANES + KWIN :] = -cosine[:, :1]
    x_wide = np.concatenate([x_rows, np.zeros((ROW_PAD, 2 * LANES - box), np.float32)], axis=1)
    return jnp.asarray(np.concatenate([y_rows, x_wide]), jnp.bfloat16)


def mirror_matrix():
    row = lax.broadcasted_iota(jnp.int32, (LANES, LANES), 0)
    col = lax.broadcasted_iota(jnp.int32, (LANES, LANES), 1)
    value = jnp.where(col < KWIN, 1.0, -1.0)
    hit = (row % KWIN + col % KWIN == KWIN) & (row // KWIN == col // KWIN)
    return jnp.where(hit, value, 0.0).astype(jnp.bfloat16)


def lane_q(shape):
    return lax.broadcasted_iota(jnp.int32, shape, 1) % KWIN


def full_spec(shape):
    return pl.BlockSpec(shape, lambda *_: (0,) * len(shape))


def params(megabytes=16):
    return pltpu.CompilerParams(vmem_limit_bytes=megabytes * 1024 * 1024)


def group(k):
    return slice(k * LANES, (k + 1) * LANES)


def fold_kernel(r_ref, *outs):
    rows = r_ref.shape[0]
    q = lane_q((rows, LANES))
    mirror = mirror_matrix()
    flip = lambda v: jnp.dot(v, mirror, preferred_element_type=jnp.float32)

    def put(k, value):
        out_ref, at = (outs[0], k) if k < CUT else (outs[1], k - CUT)
        out_ref[:, group(at)] = value.astype(out_ref.dtype)

    put(0, r_ref[:, group(0)])
    centre = r_ref[:, group(HALF)]
    special = centre.astype(jnp.float32)
    special = special + jnp.where((q >= 1) & (q < HALF), flip(centre), 0.0)
    for k in range(1, HALF):
        other = r_ref[:, group(KWIN - k)]
        put(k, r_ref[:, group(k)].astype(jnp.float32) + flip(other))
        edge = pltpu.roll(other.astype(jnp.float32), KWIN - k, 1)
        special = jnp.where(q == KWIN - k, edge, special)
    put(HALF, special)


def fold(references):
    rows = references.shape[0]
    return pl.pallas_call(
        fold_kernel,
        out_shape=[jax.ShapeDtypeStruct((rows, width), jnp.bfloat16) for width in WIDTHS],
        compiler_params=params(),
        name="fold",
    )(references)


def unfold_kernel(*rest):
    terms, (result_ref, out_ref, sems) = rest[:-3], rest[-3:]
    rows = out_ref.shape[0]
    q = lane_q((rows, LANES))
    mirror = mirror_matrix()
    count = len(terms) // 2
    chunk = 8
    width = chunk * LANES

    def copy(n):
        lanes = pl.ds(n * width, width)
        return pltpu.make_async_copy(out_ref.at[:, lanes], result_ref.at[:, lanes], sems.at[n])

    def total(k):
        chosen, at = (terms[:count], k) if k < CUT else (terms[count:], k - CUT)
        return sum(t[:, group(at)].astype(jnp.float32) for t in chosen)

    def flip(v):
        high = v.astype(jnp.bfloat16)
        low = (v - high.astype(jnp.float32)).astype(jnp.bfloat16)
        return jnp.dot(high, mirror, preferred_element_type=jnp.float32) + jnp.dot(
            low, mirror, preferred_element_type=jnp.float32
        )

    special = total(HALF)
    out_ref[:, group(0)] = total(0)
    out_ref[:, group(HALF)] = jnp.where(q <= HALF, special, flip(special))
    for k in range(1, HALF):
        value = total(k)
        out_ref[:, group(k)] = value
        edge = pltpu.roll(special, LANES - (KWIN - k), 1)
        out_ref[:, group(KWIN - k)] = jnp.where(q == 0, edge, flip(value))
        if (k + 1) % chunk == 0:
            copy(k // chunk).start()
        if k % chunk == 0:
            copy((KWIN - k) // chunk).start()
    copy(HALF // chunk).start()
    for n in range(KWIN // chunk):
        copy(n).wait()


def unfold(left, right):
    terms = list(left) + list(right)
    rows = terms[0].shape[0]
    return pl.pallas_call(
        unfold_kernel,
        in_specs=[pl.BlockSpec(memory_space=pltpu.VMEM)] * len(terms),
        out_specs=pl.BlockSpec(memory_space=pl.ANY),
        out_shape=jax.ShapeDtypeStruct((rows, KWIN * LANES), jnp.float32),
        scratch_shapes=[
            pltpu.VMEM((rows, KWIN * LANES), jnp.float32),
            pltpu.SemaphoreType.DMA((KWIN // 8,)),
        ],
        compiler_params=params(),
        name="unfold",
    )(*terms)


def dft_kernel(tile, first, table_ref, img_ref, *rest):
    out_ref, pixel_scratch, rows_scratch, lhs_scratch, sems = rest[-5:]
    tiles, box = pixel_scratch.shape[0], img_ref.shape[1]
    kept = out_ref.shape[0] - tiles * tile

    def copy(n):
        return pltpu.make_async_copy(
            img_ref.at[pl.ds(first + n * tile, tile)], pixel_scratch.at[n], sems.at[n]
        )

    for n in range(tiles):
        copy(n).start()
    if kept:
        out_ref[:kept] = rest[0][...]
    y_rows = table_ref[: 2 * box, :]
    x_rows = table_ref[2 * box :, :box]
    q = lane_q((tile, LANES))
    step, batch = 8, 11

    def one(n, carry):
        copy(n).wait()
        for start in range(0, tile, step):
            pixels = pixel_scratch[n, start : start + step].reshape(step * box, box)
            h = lax.dot_general(
                x_rows, pixels, (((1,), (1,)), ((), ())), preferred_element_type=jnp.float32
            )
            for i in range(step):
                at = (start + i) * ROW_PAD
                rows_scratch[at : at + ROW_PAD, :] = h[:, i * box : (i + 1) * box]
        for k in range(HALF + 1):
            for c in range(2):
                j = c * (HALF + 1) + k
                picked = rows_scratch[pl.ds(j, tile, stride=ROW_PAD), :]
                lhs_scratch[k * tile : (k + 1) * tile, c * box : (c + 1) * box] = picked.astype(jnp.bfloat16)
        here = pl.ds(pl.multiple_of(kept + n * tile, tile), tile)
        special = jnp.zeros((tile, LANES), jnp.float32)
        for k in range(HALF + 1):
            if k % batch == 0:
                many = jnp.dot(
                    lhs_scratch[k * tile : (k + batch) * tile, :], y_rows, preferred_element_type=jnp.float32
                )
            both = many[(k % batch) * tile : (k % batch + 1) * tile]
            value = both[:, :LANES]
            if k < HALF:
                out_ref[here, group(k)] = value.astype(jnp.bfloat16)
            else:
                special = jnp.where(q <= HALF, value, special)
            if 0 < k < HALF:
                special = jnp.where(q == KWIN - k, both[:, LANES:], special)
        out_ref[here, group(HALF)] = special.astype(jnp.bfloat16)
        return carry

    lax.fori_loop(0, tiles, one, 0)


def dft(images, table, tile, first, count, before=()):
    box = images.shape[1]
    total = count + sum(b.shape[0] for b in before)
    return pl.pallas_call(
        functools.partial(dft_kernel, tile, first),
        in_specs=[pl.BlockSpec(memory_space=pltpu.VMEM), pl.BlockSpec(memory_space=pl.ANY)]
        + [pl.BlockSpec(memory_space=pltpu.VMEM)] * len(before),
        out_shape=jax.ShapeDtypeStruct((total, UNIQUE), jnp.bfloat16),
        scratch_shapes=[
            pltpu.VMEM((count // tile, tile, box, box), jnp.bfloat16),
            pltpu.VMEM((tile * ROW_PAD, box), jnp.float32),
            pltpu.VMEM(((HALF + 1) * tile, 2 * box), jnp.bfloat16),
            pltpu.SemaphoreType.DMA((count // tile,)),
        ],
        cost_estimate=pl.CostEstimate(
            flops=count * (2 * box * box * ROW_PAD + 2 * (HALF + 1) * 2 * box * LANES * 2),
            bytes_accessed=2 * count * (box * box + UNIQUE),
            transcendentals=0,
        ),
        compiler_params=params(46),
        name="dft",
    )(table, images, *before)


def stacked_rows(at, base_ref, rows, particles):
    parts = [
        lax.broadcasted_iota(jnp.int32, (rows, particles), 0) + base_ref[n] for n in at
    ]
    return jnp.concatenate(parts, axis=0) if len(parts) > 1 else parts[0]


def stacked_rows(at, base_ref, rows, particles):
    parts = [
        lax.broadcasted_iota(jnp.int32, (rows, particles), 0) + base_ref[n] for n in at
    ]
    return jnp.concatenate(parts, axis=0) if len(parts) > 1 else parts[0]


def score_kernel(items, halves, base_ref, panel_ref, before_ref, *rest):
    specs, refs, out_ref = rest[:halves], list(rest[halves:-1]), rest[-1]
    rows = refs[0].shape[0]
    taken = []
    for at, first, width in items:
        blocks = [refs.pop(0)[...] for _ in at]
        taken.append((at, first, width, jnp.concatenate(blocks, axis=0) if len(blocks) > 1 else blocks[0]))
    edge = 0
    for spec_ref in specs:
        particles = spec_ref.shape[0]
        lanes = slice(edge, edge + particles)
        edge += particles
        picked = [before_ref[t : t + 1, lanes] for t in range(TOP)]
        for at, first, width, block in taken:
            s = lax.dot_general(
                block,
                spec_ref[:, first : first + width],
                (((1,), (1,)), ((), ())),
                preferred_element_type=jnp.float32,
            )
            row = stacked_rows(at, base_ref, rows, particles)
            for t in range(TOP):
                hit = row == panel_ref[t : t + 1, lanes]
                picked[t] = picked[t] + jnp.sum(jnp.where(hit, s, 0.0), axis=0, keepdims=True)
        for t in range(TOP):
            out_ref[t : t + 1, lanes] = picked[t]


def score(bases, spectra, panel, before, items):
    rows = items[0][2][0].shape[0]
    refs = [r for _, _, blocks in items for r in blocks]
    values = sum(r.shape[1] for r in refs) * rows
    shapes = [(at, first, blocks[0].shape[1]) for at, first, blocks in items]
    return pl.pallas_call(
        functools.partial(score_kernel, shapes, len(spectra)),
        in_specs=[pl.BlockSpec(memory_space=pltpu.SMEM)]
        + [pl.BlockSpec(memory_space=pltpu.VMEM)] * (2 + len(spectra) + len(refs)),
        out_shape=jax.ShapeDtypeStruct(panel.shape, jnp.float32),
        cost_estimate=pl.CostEstimate(
            flops=2 * values * panel.shape[1], bytes_accessed=2 * values, transcendentals=0
        ),
        compiler_params=params(),
        name="score",
    )(bases, panel, before, *spectra, *refs)


def weight_kernel(*rest):
    (prior_ref, precision_ref, out_ref), scores = rest[-3:], rest[:-3]
    total = scores[0][...]
    for ref in scores[1:]:
        total = total + ref[...]
    value = total * precision_ref[...]
    unscaled = prior_ref[...] * jnp.exp(value - jnp.max(value, axis=0, keepdims=True))
    weight = unscaled / jnp.sum(unscaled, axis=0, keepdims=True)
    out_ref[...] = weight.astype(jnp.bfloat16).astype(jnp.float32)


def weights_of(scores, prior, precision):
    return pl.pallas_call(
        weight_kernel,
        out_shape=jax.ShapeDtypeStruct(prior.shape, jnp.float32),
        compiler_params=params(),
        name="weights",
    )(*scores, prior, precision)


def sums_kernel(items, halves, base_ref, weight_ref, panel_ref, *rest):
    specs, outs = rest[:halves], list(rest[halves:])
    particles = panel_ref.shape[1]
    for at, first in items:
        rows, width = outs[0].shape
        row = stacked_rows(at, base_ref, rows, particles)
        select = jnp.zeros(row.shape, jnp.float32)
        for t in range(TOP):
            select = select + jnp.where(row == panel_ref[t : t + 1, :], weight_ref[t : t + 1, :], 0.0)
        select = select.astype(jnp.bfloat16)
        total, edge = None, 0
        for spec_ref in specs:
            count = spec_ref.shape[0]
            term = jnp.dot(
                select[:, edge : edge + count],
                spec_ref[:, first : first + width],
                preferred_element_type=jnp.float32,
            )
            total = term if total is None else total + term
            edge += count
        for n in range(len(at)):
            out_ref = outs.pop(0)
            out_ref[...] = total[n * rows : (n + 1) * rows].astype(out_ref.dtype)


def sums(bases, weight, panel, spectra, rows, items, dtype):
    particles = panel.shape[1]
    shapes = [(rows, width) for at, _, width in items for _ in at]
    values = sum(a * b for a, b in shapes)
    return pl.pallas_call(
        functools.partial(sums_kernel, [(at, first) for at, first, _ in items], len(spectra)),
        in_specs=[pl.BlockSpec(memory_space=pltpu.SMEM)]
        + [pl.BlockSpec(memory_space=pltpu.VMEM)] * (2 + len(spectra)),
        out_shape=[jax.ShapeDtypeStruct(shape, dtype) for shape in shapes],
        cost_estimate=pl.CostEstimate(
            flops=2 * values * particles, bytes_accessed=4 * values, transcendentals=0
        ),
        compiler_params=params(),
        name="sums",
    )(bases, weight, panel, *spectra)


RING = (0, 2, 4, 6, 7, 5, 3, 1)


def ring_places():
    count = len(RING)
    table = np.zeros((count, count), np.int32)
    for at, place in enumerate(RING):
        table[place] = [RING[(at + d) % count] for d in range(count)]
    return table


def onward(value):
    return lax.ppermute(value, "dp", list(zip(RING, RING[1:] + RING[:1])))


def backward(value):
    return lax.ppermute(value, "dp", list(zip(RING[1:] + RING[:1], RING)))


def tie(*values):
    return lax.optimization_barrier(values)


def by_ring(images, references, panel, prior, precision):
    rows = references.shape[0]
    cls_count = lax.axis_size("cls")
    place, mine = lax.axis_index("dp"), lax.axis_index("cls")
    table = half_tables(images.shape[1])
    bases = (jnp.asarray(ring_places())[place] * cls_count + mine) * rows
    starts = (0, WIDTHS[0])

    own = fold(references)
    p1 = onward(own[0]), backward(own[1])
    q1 = onward(own[1]), backward(own[0])
    half = images.shape[0] // 2
    left = dft(images, table, 64, 0, half)
    *p1, left, table = tie(*p1, left, table)
    p2 = onward(p1[0]), backward(p1[1])
    *q1, table = tie(*q1, table)
    q2 = onward(q1[0]), backward(q1[1])
    right = dft(images, table, 64, half, half // 2)
    *p2, right, table = tie(*p2, right, table)
    p3 = onward(p2[0]), backward(p2[1])
    *q2, table = tie(*q2, table)
    q3 = onward(q2[0]), backward(q2[1])
    right = dft(images, table, 64, half + half // 2, half // 2, [right])
    spectra = [left, right]
    *p3, right = tie(*p3, right)
    spectra = [left, right]
    p4 = onward(p3[0]), backward(p3[1])
    picked = jnp.zeros(panel.shape, jnp.float32)
    near = [
        ((0, 7, 1), starts[0], [own[0], p1[0], q1[1]]),
        ((0, 7, 1), starts[1], [own[1], q1[0], p1[1]]),
        ((6, 2), starts[0], [p2[0], q2[1]]),
        ((6, 2), starts[1], [q2[0], p2[1]]),
    ]
    picked = score(bases, spectra, panel, picked, near)
    *q3, picked = tie(*q3, picked)
    middle = [((5, 3), starts[0], [p3[0], q3[1]]), ((5, 3), starts[1], [q3[0], p3[1]])]
    picked = score(bases, spectra, panel, picked, middle)
    *p4, picked = tie(*p4, picked)
    picked = score(bases, spectra, panel, picked, [((4,), starts[p], [p4[p]]) for p in range(2)])

    turns = [[(c, c ^ n) for c in range(cls_count)] for n in range(1, cls_count)]
    scores = [picked] + [lax.ppermute(picked, "cls", turn) for turn in turns]
    weight = weights_of(scores, prior, precision)

    narrow, wide = jnp.bfloat16, jnp.float32
    part = functools.partial(sums, bases, weight, panel, spectra, rows)
    pieces = [(starts[p], WIDTHS[p]) for p in range(2)]
    far0, back0, far1, ahead1 = part([((4, 5), *pieces[0]), ((4, 3), *pieces[1])], narrow)
    p = onward(far0), backward(far1)
    q = onward(ahead1), backward(back0)
    rest = part([((3, 2, 6, 1, 7, 0), *pieces[0]), ((5, 2, 6, 1, 7, 0), *pieces[1])], wide)

    def pass_on(arrived, held):
        onto = [(h + a.astype(wide)).astype(narrow) for h, a in zip(held, arrived)]
        return onward(onto[0]), backward(onto[1])

    p = tie(*p)
    p = pass_on(p, (rest[0], rest[6]))
    q = pass_on(q, (rest[7], rest[2]))
    p = pass_on(p, (rest[1], rest[8]))
    q = pass_on(q, (rest[9], rest[4]))
    p = pass_on(p, (rest[3], rest[10]))
    return unfold([rest[5], p[0], q[1]], [rest[11], q[0], p[1]])


def by_collectives(images, references, panel, prior, precision):
    rows = references.shape[0]
    dp_count = lax.axis_size("dp")
    cls_count = lax.axis_size("cls")
    mine = lax.axis_index("cls")
    table = half_tables(images.shape[1])
    own = jnp.concatenate(fold(references), axis=1)
    gathered = lax.all_gather(own, "dp", axis=0, tiled=False)
    half = images.shape[0] // 2
    spectra = [dft(images, table, 64, part * half, half) for part in range(2)]
    bases = (jnp.arange(dp_count, dtype=jnp.int32) * cls_count + mine) * rows
    picked = jnp.zeros(panel.shape, jnp.float32)
    items = [((n,), 0, [gathered[n]]) for n in range(dp_count)]
    for start in range(0, dp_count, 8):
        picked = score(bases, spectra, panel, picked, items[start : start + 8])
    scores = lax.all_gather(picked, "cls", axis=0, tiled=False)
    weight = weights_of([scores[n] for n in range(cls_count)], prior, precision)
    partial = []
    for start in range(0, dp_count, 8):
        items = [((n,), 0, UNIQUE) for n in range(start, min(start + 8, dp_count))]
        partial += sums(bases, weight, panel, spectra, rows, items, jnp.bfloat16)
    half = lax.psum_scatter(jnp.stack(partial), "dp", scatter_dimension=0, tiled=False)
    return unfold([half[:, : WIDTHS[0]]], [half[:, WIDTHS[0] :]])


def on_device(images, references, best_class, best_rot, prior, precision):
    panel = (best_class * ROTS + best_rot).T
    plan = by_ring if lax.axis_size("dp") == len(RING) else by_collectives
    return plan(images, references, panel, prior.T, precision[None, :])


def solution(mesh):
    in_specs = (
        P("dp", None, None),
        P(("dp", "cls"), None),
        P("dp", None),
        P("dp", None),
        P("dp", None),
        P("dp"),
    )
    out_specs = P(("dp", "cls"), None)
    return jax.shard_map(on_device, mesh=mesh, in_specs=in_specs, out_specs=out_specs, check_vma=False)
```

```python
import functools
import math

import numpy as np
import jax
import jax.numpy as jnp
from jax import lax
from jax.experimental import pallas as pl
from jax.experimental.pallas import tpu as pltpu
from jax.sharding import PartitionSpec as P

KWIN = 64
HALF = KWIN // 2
ROTS = 36
TOP = 4
LANES = 2 * KWIN
UNIQUE = (HALF + 1) * LANES
ROW_PAD = 72
CUT = 17
WIDTHS = (CUT * LANES, UNIQUE - CUT * LANES)


def half_tables(box):
    positions = np.arange(box, dtype=np.float32)
    frequencies = np.arange(KWIN, dtype=np.float32) - float(HALF)
    phase_x = (2.0 * math.pi * positions[:, None] * frequencies[None, : HALF + 1] / box).astype(np.float32)
    x_rows = np.zeros((ROW_PAD, box), np.float32)
    x_rows[: HALF + 1] = np.cos(phase_x).T / box
    x_rows[HALF + 1 : 2 * HALF + 2] = -np.sin(phase_x).T / box
    angle = (2.0 * math.pi * positions[:, None] * frequencies[None, :] / box).astype(np.float32)
    cosine, sine = np.cos(angle), np.sin(angle)
    y_rows = np.zeros((2 * box, 2 * LANES), np.float32)
    y_rows[:box, :KWIN] = cosine
    y_rows[:box, KWIN:LANES] = -sine
    y_rows[box:, :KWIN] = sine
    y_rows[box:, KWIN:LANES] = cosine
    y_rows[:box, LANES : LANES + KWIN] = cosine[:, :1]
    y_rows[:box, LANES + KWIN :] = -sine[:, :1]
    y_rows[box:, LANES : LANES + KWIN] = -sine[:, :1]
    y_rows[box:, LANES + KWIN :] = -cosine[:, :1]
    x_wide = np.concatenate([x_rows, np.zeros((ROW_PAD, 2 * LANES - box), np.float32)], axis=1)
    return jnp.asarray(np.concatenate([y_rows, x_wide]), jnp.bfloat16)


def mirror_matrix():
    row = lax.broadcasted_iota(jnp.int32, (LANES, LANES), 0)
    col = lax.broadcasted_iota(jnp.int32, (LANES, LANES), 1)
    value = jnp.where(col < KWIN, 1.0, -1.0)
    hit = (row % KWIN + col % KWIN == KWIN) & (row // KWIN == col // KWIN)
    return jnp.where(hit, value, 0.0).astype(jnp.bfloat16)


def lane_q(shape):
    return lax.broadcasted_iota(jnp.int32, shape, 1) % KWIN


def full_spec(shape):
    return pl.BlockSpec(shape, lambda *_: (0,) * len(shape))


def params(megabytes=16):
    return pltpu.CompilerParams(vmem_limit_bytes=megabytes * 1024 * 1024)


def group(k):
    return slice(k * LANES, (k + 1) * LANES)


def fold_kernel(r_ref, *outs):
    rows = r_ref.shape[0]
    q = lane_q((rows, LANES))
    mirror = mirror_matrix()
    flip = lambda v: jnp.dot(v, mirror, preferred_element_type=jnp.float32)

    def put(k, value):
        out_ref, at = (outs[0], k) if k < CUT else (outs[1], k - CUT)
        out_ref[:, group(at)] = value.astype(out_ref.dtype)

    put(0, r_ref[:, group(0)])
    centre = r_ref[:, group(HALF)]
    special = centre.astype(jnp.float32)
    special = special + jnp.where((q >= 1) & (q < HALF), flip(centre), 0.0)
    for k in range(1, HALF):
        other = r_ref[:, group(KWIN - k)]
        put(k, r_ref[:, group(k)].astype(jnp.float32) + flip(other))
        edge = pltpu.roll(other.astype(jnp.float32), KWIN - k, 1)
        special = jnp.where(q == KWIN - k, edge, special)
    put(HALF, special)


def fold(references):
    rows = references.shape[0]
    return pl.pallas_call(
        fold_kernel,
        out_shape=[jax.ShapeDtypeStruct((rows, width), jnp.bfloat16) for width in WIDTHS],
        compiler_params=params(),
        name="fold",
    )(references)


def unfold_kernel(*rest):
    terms, (result_ref, out_ref, sems) = rest[:-3], rest[-3:]
    rows = out_ref.shape[0]
    q = lane_q((rows, LANES))
    mirror = mirror_matrix()
    count = len(terms) // 2
    chunk = 8
    width = chunk * LANES

    def copy(n):
        lanes = pl.ds(n * width, width)
        return pltpu.make_async_copy(out_ref.at[:, lanes], result_ref.at[:, lanes], sems.at[n])

    def total(k):
        chosen, at = (terms[:count], k) if k < CUT else (terms[count:], k - CUT)
        return sum(t[:, group(at)].astype(jnp.float32) for t in chosen)

    twice = jnp.concatenate([mirror, mirror], axis=0)

    def flip(v):
        high = v.astype(jnp.bfloat16)
        low = (v - high.astype(jnp.float32)).astype(jnp.bfloat16)
        return jnp.dot(
            jnp.concatenate([high, low], axis=1), twice, preferred_element_type=jnp.float32
        )

    special = total(HALF)
    out_ref[:, group(0)] = total(0)
    out_ref[:, group(HALF)] = jnp.where(q <= HALF, special, flip(special))
    for k in range(1, HALF):
        if k % chunk == 1:
            values = [total(n) for n in range(k, min(k + chunk, HALF))]
            flipped = flip(jnp.concatenate(values, axis=0))
        at = (k - 1) % chunk
        out_ref[:, group(k)] = values[at]
        edge = pltpu.roll(special, LANES - (KWIN - k), 1)
        out_ref[:, group(KWIN - k)] = jnp.where(q == 0, edge, flipped[at * rows : (at + 1) * rows])
        if (k + 1) % chunk == 0:
            copy(k // chunk).start()
        if k % chunk == 0:
            copy((KWIN - k) // chunk).start()
    copy(HALF // chunk).start()
    for n in range(KWIN // chunk):
        copy(n).wait()


def unfold(left, right):
    terms = list(left) + list(right)
    rows = terms[0].shape[0]
    return pl.pallas_call(
        unfold_kernel,
        in_specs=[pl.BlockSpec(memory_space=pltpu.VMEM)] * len(terms),
        out_specs=pl.BlockSpec(memory_space=pl.ANY),
        out_shape=jax.ShapeDtypeStruct((rows, KWIN * LANES), jnp.float32),
        scratch_shapes=[
            pltpu.VMEM((rows, KWIN * LANES), jnp.float32),
            pltpu.SemaphoreType.DMA((KWIN // 8,)),
        ],
        compiler_params=params(),
        name="unfold",
    )(*terms)


def dft_kernel(tile, first, table_ref, img_ref, *rest):
    out_ref, pixel_scratch, rows_scratch, lhs_scratch, sems = rest[-5:]
    tiles, box = pixel_scratch.shape[0], img_ref.shape[1]
    kept = out_ref.shape[0] - tiles * tile

    def copy(n):
        return pltpu.make_async_copy(
            img_ref.at[pl.ds(first + n * tile, tile)], pixel_scratch.at[n], sems.at[n]
        )

    for n in range(tiles):
        copy(n).start()
    if kept:
        out_ref[:kept] = rest[0][...]
    y_rows = table_ref[: 2 * box, :]
    x_rows = table_ref[2 * box :, :box]
    q = lane_q((tile, LANES))
    step, batch = 8, 11

    def one(n, carry):
        copy(n).wait()
        for start in range(0, tile, step):
            pixels = pixel_scratch[n, start : start + step].reshape(step * box, box)
            h = lax.dot_general(
                x_rows, pixels, (((1,), (1,)), ((), ())), preferred_element_type=jnp.float32
            )
            for i in range(step):
                at = (start + i) * ROW_PAD
                rows_scratch[at : at + ROW_PAD, :] = h[:, i * box : (i + 1) * box]
        for k in range(HALF + 1):
            for c in range(2):
                j = c * (HALF + 1) + k
                picked = rows_scratch[pl.ds(j, tile, stride=ROW_PAD), :]
                lhs_scratch[k * tile : (k + 1) * tile, c * box : (c + 1) * box] = picked.astype(jnp.bfloat16)
        here = pl.ds(pl.multiple_of(kept + n * tile, tile), tile)
        special = jnp.zeros((tile, LANES), jnp.float32)
        for k in range(HALF + 1):
            if k % batch == 0:
                many = jnp.dot(
                    lhs_scratch[k * tile : (k + batch) * tile, :], y_rows, preferred_element_type=jnp.float32
                )
            both = many[(k % batch) * tile : (k % batch + 1) * tile]
            value = both[:, :LANES]
            if k < HALF:
                out_ref[here, group(k)] = value.astype(jnp.bfloat16)
            else:
                special = jnp.where(q <= HALF, value, special)
            if 0 < k < HALF:
                special = jnp.where(q == KWIN - k, both[:, LANES:], special)
        out_ref[here, group(HALF)] = special.astype(jnp.bfloat16)
        return carry

    lax.fori_loop(0, tiles, one, 0)


def dft(images, table, tile, first, count, before=()):
    box = images.shape[1]
    total = count + sum(b.shape[0] for b in before)
    return pl.pallas_call(
        functools.partial(dft_kernel, tile, first),
        in_specs=[pl.BlockSpec(memory_space=pltpu.VMEM), pl.BlockSpec(memory_space=pl.ANY)]
        + [pl.BlockSpec(memory_space=pltpu.VMEM)] * len(before),
        out_shape=jax.ShapeDtypeStruct((total, UNIQUE), jnp.bfloat16),
        scratch_shapes=[
            pltpu.VMEM((count // tile, tile, box, box), jnp.bfloat16),
            pltpu.VMEM(((tile + 1) * ROW_PAD, box), jnp.float32),
            pltpu.VMEM(((HALF + 1) * tile, 2 * box), jnp.bfloat16),
            pltpu.SemaphoreType.DMA((count // tile,)),
        ],
        cost_estimate=pl.CostEstimate(
            flops=count * (2 * box * box * ROW_PAD + 2 * (HALF + 1) * 2 * box * LANES * 2),
            bytes_accessed=2 * count * (box * box + UNIQUE),
            transcendentals=0,
        ),
        compiler_params=params(46),
        name="dft",
    )(table, images, *before)


def stacked_rows(at, base_ref, rows, particles):
    parts = [
        lax.broadcasted_iota(jnp.int32, (rows, particles), 0) + base_ref[n] for n in at
    ]
    return jnp.concatenate(parts, axis=0) if len(parts) > 1 else parts[0]


def stacked_rows(at, base_ref, rows, particles):
    parts = [
        lax.broadcasted_iota(jnp.int32, (rows, particles), 0) + base_ref[n] for n in at
    ]
    return jnp.concatenate(parts, axis=0) if len(parts) > 1 else parts[0]


def score_kernel(items, halves, base_ref, panel_ref, before_ref, *rest):
    specs, refs, out_ref = rest[:halves], list(rest[halves:-1]), rest[-1]
    rows = refs[0].shape[0]
    taken = []
    for at, first, width in items:
        blocks = [refs.pop(0)[...] for _ in at]
        taken.append((at, first, width, jnp.concatenate(blocks, axis=0) if len(blocks) > 1 else blocks[0]))
    edge = 0
    for spec_ref in specs:
        particles = spec_ref.shape[0]
        lanes = slice(edge, edge + particles)
        edge += particles
        picked = [before_ref[t : t + 1, lanes] for t in range(TOP)]
        for at, first, width, block in taken:
            s = lax.dot_general(
                block,
                spec_ref[:, first : first + width],
                (((1,), (1,)), ((), ())),
                preferred_element_type=jnp.float32,
            )
            row = stacked_rows(at, base_ref, rows, particles)
            for t in range(TOP):
                hit = row == panel_ref[t : t + 1, lanes]
                picked[t] = picked[t] + jnp.sum(jnp.where(hit, s, 0.0), axis=0, keepdims=True)
        for t in range(TOP):
            out_ref[t : t + 1, lanes] = picked[t]


def score(bases, spectra, panel, before, items):
    rows = items[0][2][0].shape[0]
    refs = [r for _, _, blocks in items for r in blocks]
    values = sum(r.shape[1] for r in refs) * rows
    shapes = [(at, first, blocks[0].shape[1]) for at, first, blocks in items]
    return pl.pallas_call(
        functools.partial(score_kernel, shapes, len(spectra)),
        in_specs=[pl.BlockSpec(memory_space=pltpu.SMEM)]
        + [pl.BlockSpec(memory_space=pltpu.VMEM)] * (2 + len(spectra) + len(refs)),
        out_shape=jax.ShapeDtypeStruct(panel.shape, jnp.float32),
        cost_estimate=pl.CostEstimate(
            flops=2 * values * panel.shape[1], bytes_accessed=2 * values, transcendentals=0
        ),
        compiler_params=params(),
        name="score",
    )(bases, panel, before, *spectra, *refs)


def softmax(score_refs, prior_ref, precision_ref):
    total = score_refs[0][...]
    for ref in score_refs[1:]:
        total = total + ref[...]
    value = total * precision_ref[...]
    unscaled = prior_ref[...] * jnp.exp(value - jnp.max(value, axis=0, keepdims=True))
    weight = unscaled / jnp.sum(unscaled, axis=0, keepdims=True)
    return weight.astype(jnp.bfloat16).astype(jnp.float32)


def sums_kernel(items, halves, count, base_ref, panel_ref, *rest):
    specs, given, outs = rest[:halves], rest[halves : halves + count], list(rest[halves + count :])
    particles = panel_ref.shape[1]
    if count == 1:
        weight_ref = given[0]
    else:
        weight_ref = outs.pop(0)
        weight_ref[...] = softmax(given[:-2], *given[-2:])
    for at, first in items:
        rows, width = outs[0].shape
        row = stacked_rows(at, base_ref, rows, particles)
        select = jnp.zeros(row.shape, jnp.float32)
        for t in range(TOP):
            select = select + jnp.where(row == panel_ref[t : t + 1, :], weight_ref[t : t + 1, :], 0.0)
        select = select.astype(jnp.bfloat16)
        total, edge = None, 0
        for spec_ref in specs:
            count = spec_ref.shape[0]
            term = jnp.dot(
                select[:, edge : edge + count],
                spec_ref[:, first : first + width],
                preferred_element_type=jnp.float32,
            )
            total = term if total is None else total + term
            edge += count
        for n in range(len(at)):
            out_ref = outs.pop(0)
            out_ref[...] = total[n * rows : (n + 1) * rows].astype(out_ref.dtype)


def sums(bases, weight, panel, spectra, rows, items, dtype):
    particles = panel.shape[1]
    given = list(weight) if isinstance(weight, (list, tuple)) else [weight]
    shapes = [(rows, width) for at, _, width in items for _ in at]
    values = sum(a * b for a, b in shapes)
    out_shape = [jax.ShapeDtypeStruct(shape, dtype) for shape in shapes]
    if len(given) > 1:
        out_shape = [jax.ShapeDtypeStruct(panel.shape, jnp.float32)] + out_shape
    return pl.pallas_call(
        functools.partial(sums_kernel, [(at, first) for at, first, _ in items], len(spectra), len(given)),
        in_specs=[pl.BlockSpec(memory_space=pltpu.SMEM)]
        + [pl.BlockSpec(memory_space=pltpu.VMEM)] * (1 + len(spectra) + len(given)),
        out_shape=out_shape,
        cost_estimate=pl.CostEstimate(
            flops=2 * values * particles, bytes_accessed=4 * values, transcendentals=0
        ),
        compiler_params=params(),
        name="sums",
    )(bases, panel, *spectra, *given)


RING = (0, 2, 4, 6, 7, 5, 3, 1)


def ring_places():
    count = len(RING)
    table = np.zeros((count, count), np.int32)
    for at, place in enumerate(RING):
        table[place] = [RING[(at + d) % count] for d in range(count)]
    return table


def onward(value):
    return lax.ppermute(value, "dp", list(zip(RING, RING[1:] + RING[:1])))


def backward(value):
    return lax.ppermute(value, "dp", list(zip(RING[1:] + RING[:1], RING)))


def tie(*values):
    return lax.optimization_barrier(values)


def by_ring(images, references, panel, prior, precision):
    rows = references.shape[0]
    cls_count = lax.axis_size("cls")
    place, mine = lax.axis_index("dp"), lax.axis_index("cls")
    table = half_tables(images.shape[1])
    bases = (jnp.asarray(ring_places())[place] * cls_count + mine) * rows
    starts = (0, WIDTHS[0])

    own = fold(references)
    p1 = onward(own[0]), backward(own[1])
    q1 = onward(own[1]), backward(own[0])
    half = images.shape[0] // 2
    left = dft(images, table, 64, 0, half)
    *p1, left, table = tie(*p1, left, table)
    p2 = onward(p1[0]), backward(p1[1])
    *q1, table = tie(*q1, table)
    q2 = onward(q1[0]), backward(q1[1])
    right = dft(images, table, 64, half, half // 2)
    *p2, right, table = tie(*p2, right, table)
    p3 = onward(p2[0]), backward(p2[1])
    *q2, table = tie(*q2, table)
    q3 = onward(q2[0]), backward(q2[1])
    right = dft(images, table, 64, half + half // 2, half // 2, [right])
    spectra = [left, right]
    *p3, right = tie(*p3, right)
    spectra = [left, right]
    p4 = onward(p3[0]), backward(p3[1])
    picked = jnp.zeros(panel.shape, jnp.float32)
    near = [
        ((0, 7, 1), starts[0], [own[0], p1[0], q1[1]]),
        ((0, 7, 1), starts[1], [own[1], q1[0], p1[1]]),
        ((6, 2), starts[0], [p2[0], q2[1]]),
        ((6, 2), starts[1], [q2[0], p2[1]]),
    ]
    picked = score(bases, spectra, panel, picked, near)
    *q3, picked = tie(*q3, picked)
    middle = [((5, 3), starts[0], [p3[0], q3[1]]), ((5, 3), starts[1], [q3[0], p3[1]])]
    picked = score(bases, spectra, panel, picked, middle)
    *p4, picked = tie(*p4, picked)
    picked = score(bases, spectra, panel, picked, [((4,), starts[p], [p4[p]]) for p in range(2)])

    turns = [[(c, c ^ n) for c in range(cls_count)] for n in range(1, cls_count)]
    weight = [picked] + [lax.ppermute(picked, "cls", turn) for turn in turns] + [prior, precision]

    narrow, wide = jnp.bfloat16, jnp.float32
    pieces = [(starts[p], WIDTHS[p]) for p in range(2)]

    def part(places, dtype):
        items = [(at, *piece) for at, piece in zip(zip(*places), pieces)]
        return sums(bases, weight, panel, spectra, rows, items, dtype)

    def pass_on(arrived, held):
        onto = [(h + a.astype(wide)).astype(narrow) for h, a in zip(held, arrived)]
        return onward(onto[0]), backward(onto[1])

    weight, far0, back0, far1, ahead1 = part([(4, 4), (5, 3)], narrow)
    p = onward(far0), backward(far1)
    q = onward(ahead1), backward(back0)
    held = list(part([(3, 5)], wide))
    *p, weight, held[0], held[1] = tie(*p, weight, *held)
    p = pass_on(p, held)
    held = list(part([(6, 2)], wide))
    *q, weight, held[0], held[1] = tie(*q, weight, *held)
    q = pass_on(q, held[::-1])
    held = list(part([(2, 6)], wide))
    *p, weight, held[0], held[1] = tie(*p, weight, *held)
    p = pass_on(p, held)
    held = list(part([(7, 1)], wide))
    *q, weight, held[0], held[1] = tie(*q, weight, *held)
    q = pass_on(q, held[::-1])
    held = list(part([(1, 7)], wide))
    *p, weight, held[0], held[1] = tie(*p, weight, *held)
    p = pass_on(p, held)
    kept = part([(0, 0)], wide)
    return unfold([kept[0], p[0], q[1]], [kept[1], q[0], p[1]])


def by_collectives(images, references, panel, prior, precision):
    rows = references.shape[0]
    dp_count = lax.axis_size("dp")
    cls_count = lax.axis_size("cls")
    mine = lax.axis_index("cls")
    table = half_tables(images.shape[1])
    own = jnp.concatenate(fold(references), axis=1)
    gathered = lax.all_gather(own, "dp", axis=0, tiled=False)
    half = images.shape[0] // 2
    spectra = [dft(images, table, 64, part * half, half) for part in range(2)]
    bases = (jnp.arange(dp_count, dtype=jnp.int32) * cls_count + mine) * rows
    picked = jnp.zeros(panel.shape, jnp.float32)
    items = [((n,), 0, [gathered[n]]) for n in range(dp_count)]
    for start in range(0, dp_count, 8):
        picked = score(bases, spectra, panel, picked, items[start : start + 8])
    scores = lax.all_gather(picked, "cls", axis=0, tiled=False)
    weight = [scores[n] for n in range(cls_count)] + [prior, precision]
    partial = []
    for start in range(0, dp_count, 8):
        items = [((n,), 0, UNIQUE) for n in range(start, min(start + 8, dp_count))]
        made = sums(bases, weight, panel, spectra, rows, items, jnp.bfloat16)
        weight, made = (made[0], made[1:]) if start == 0 else (weight, made)
        partial += made
    half = lax.psum_scatter(jnp.stack(partial), "dp", scatter_dimension=0, tiled=False)
    return unfold([half[:, : WIDTHS[0]]], [half[:, WIDTHS[0] :]])


def on_device(images, references, best_class, best_rot, prior, precision):
    panel = (best_class * ROTS + best_rot).T
    plan = by_ring if lax.axis_size("dp") == len(RING) else by_collectives
    return plan(images, references, panel, prior.T, precision[None, :])


def solution(mesh):
    in_specs = (
        P("dp", None, None),
        P(("dp", "cls"), None),
        P("dp", None),
        P("dp", None),
        P("dp", None),
        P("dp"),
    )
    out_specs = P(("dp", "cls"), None)
    return jax.shard_map(on_device, mesh=mesh, in_specs=in_specs, out_specs=out_specs, check_vma=False)
```

```python
import functools
import math

import numpy as np
import jax
import jax.numpy as jnp
from jax import lax
from jax.experimental import pallas as pl
from jax.experimental.pallas import tpu as pltpu
from jax.sharding import PartitionSpec as P

KWIN = 64
HALF = KWIN // 2
ROTS = 36
TOP = 4
LANES = 2 * KWIN
UNIQUE = (HALF + 1) * LANES
ROW_PAD = 72
CUT = 17
WIDTHS = (CUT * LANES, UNIQUE - CUT * LANES)


def half_tables(box):
    positions = np.arange(box, dtype=np.float32)
    frequencies = np.arange(KWIN, dtype=np.float32) - float(HALF)
    phase_x = (2.0 * math.pi * positions[:, None] * frequencies[None, : HALF + 1] / box).astype(np.float32)
    x_rows = np.zeros((ROW_PAD, box), np.float32)
    x_rows[: HALF + 1] = np.cos(phase_x).T / box
    x_rows[HALF + 1 : 2 * HALF + 2] = -np.sin(phase_x).T / box
    angle = (2.0 * math.pi * positions[:, None] * frequencies[None, :] / box).astype(np.float32)
    cosine, sine = np.cos(angle), np.sin(angle)
    y_rows = np.zeros((2 * box, 2 * LANES), np.float32)
    y_rows[:box, :KWIN] = cosine
    y_rows[:box, KWIN:LANES] = -sine
    y_rows[box:, :KWIN] = sine
    y_rows[box:, KWIN:LANES] = cosine
    y_rows[:box, LANES : LANES + KWIN] = cosine[:, :1]
    y_rows[:box, LANES + KWIN :] = -sine[:, :1]
    y_rows[box:, LANES : LANES + KWIN] = -sine[:, :1]
    y_rows[box:, LANES + KWIN :] = -cosine[:, :1]
    x_wide = np.concatenate([x_rows, np.zeros((ROW_PAD, 2 * LANES - box), np.float32)], axis=1)
    return jnp.asarray(np.concatenate([y_rows, x_wide]), jnp.bfloat16)


def mirror_matrix():
    row = lax.broadcasted_iota(jnp.int32, (LANES, LANES), 0)
    col = lax.broadcasted_iota(jnp.int32, (LANES, LANES), 1)
    value = jnp.where(col < KWIN, 1.0, -1.0)
    hit = (row % KWIN + col % KWIN == KWIN) & (row // KWIN == col // KWIN)
    return jnp.where(hit, value, 0.0).astype(jnp.bfloat16)


def lane_q(shape):
    return lax.broadcasted_iota(jnp.int32, shape, 1) % KWIN


def full_spec(shape):
    return pl.BlockSpec(shape, lambda *_: (0,) * len(shape))


def params(megabytes=16):
    return pltpu.CompilerParams(vmem_limit_bytes=megabytes * 1024 * 1024)


def group(k):
    return slice(k * LANES, (k + 1) * LANES)


def fold_kernel(r_ref, *outs):
    rows = r_ref.shape[0]
    q = lane_q((rows, LANES))
    mirror = mirror_matrix()
    flip = lambda v: jnp.dot(v, mirror, preferred_element_type=jnp.float32)

    def put(k, value):
        out_ref, at = (outs[0], k) if k < CUT else (outs[1], k - CUT)
        out_ref[:, group(at)] = value.astype(out_ref.dtype)

    put(0, r_ref[:, group(0)])
    centre = r_ref[:, group(HALF)]
    special = centre.astype(jnp.float32)
    special = special + jnp.where((q >= 1) & (q < HALF), flip(centre), 0.0)
    for k in range(1, HALF):
        other = r_ref[:, group(KWIN - k)]
        put(k, r_ref[:, group(k)].astype(jnp.float32) + flip(other))
        edge = pltpu.roll(other.astype(jnp.float32), KWIN - k, 1)
        special = jnp.where(q == KWIN - k, edge, special)
    put(HALF, special)


def fold(references):
    rows = references.shape[0]
    return pl.pallas_call(
        fold_kernel,
        out_shape=[jax.ShapeDtypeStruct((rows, width), jnp.bfloat16) for width in WIDTHS],
        compiler_params=params(),
        name="fold",
    )(references)


def unfold_kernel(*rest):
    terms, (result_ref, out_ref, sems) = rest[:-3], rest[-3:]
    rows = out_ref.shape[0]
    q = lane_q((rows, LANES))
    mirror = mirror_matrix()
    count = len(terms) // 2
    chunk = 8
    width = chunk * LANES

    def copy(n):
        lanes = pl.ds(n * width, width)
        return pltpu.make_async_copy(out_ref.at[:, lanes], result_ref.at[:, lanes], sems.at[n])

    def total(k):
        chosen, at = (terms[:count], k) if k < CUT else (terms[count:], k - CUT)
        return sum(t[:, group(at)].astype(jnp.float32) for t in chosen)

    twice = jnp.concatenate([mirror, mirror], axis=0)

    def flip(v):
        high = v.astype(jnp.bfloat16)
        low = (v - high.astype(jnp.float32)).astype(jnp.bfloat16)
        return jnp.dot(
            jnp.concatenate([high, low], axis=1), twice, preferred_element_type=jnp.float32
        )

    special = total(HALF)
    out_ref[:, group(0)] = total(0)
    out_ref[:, group(HALF)] = jnp.where(q <= HALF, special, flip(special))
    for k in range(1, HALF):
        if k % chunk == 1:
            values = [total(n) for n in range(k, min(k + chunk, HALF))]
            flipped = flip(jnp.concatenate(values, axis=0))
        at = (k - 1) % chunk
        out_ref[:, group(k)] = values[at]
        edge = pltpu.roll(special, LANES - (KWIN - k), 1)
        out_ref[:, group(KWIN - k)] = jnp.where(q == 0, edge, flipped[at * rows : (at + 1) * rows])
        if (k + 1) % chunk == 0:
            copy(k // chunk).start()
        if k % chunk == 0:
            copy((KWIN - k) // chunk).start()
    copy(HALF // chunk).start()
    for n in range(KWIN // chunk):
        copy(n).wait()


def unfold(left, right):
    terms = list(left) + list(right)
    rows = terms[0].shape[0]
    return pl.pallas_call(
        unfold_kernel,
        in_specs=[pl.BlockSpec(memory_space=pltpu.VMEM)] * len(terms),
        out_specs=pl.BlockSpec(memory_space=pl.ANY),
        out_shape=jax.ShapeDtypeStruct((rows, KWIN * LANES), jnp.float32),
        scratch_shapes=[
            pltpu.VMEM((rows, KWIN * LANES), jnp.float32),
            pltpu.SemaphoreType.DMA((KWIN // 8,)),
        ],
        compiler_params=params(),
        name="unfold",
    )(*terms)


def dft_kernel(tile, first, table_ref, img_ref, *rest):
    out_ref, pixel_scratch, rows_scratch, lhs_scratch, sems = rest[-5:]
    tiles, box = pixel_scratch.shape[0], img_ref.shape[1]
    kept = out_ref.shape[0] - tiles * tile

    def copy(n):
        return pltpu.make_async_copy(
            img_ref.at[pl.ds(first + n * tile, tile)], pixel_scratch.at[n], sems.at[n]
        )

    for n in range(tiles):
        copy(n).start()
    if kept:
        out_ref[:kept] = rest[0][...]
    y_rows = table_ref[: 2 * box, :]
    x_rows = table_ref[2 * box :, :box]
    q = lane_q((tile, LANES))
    step, batch = 8, 11

    def one(n, carry):
        copy(n).wait()
        for start in range(0, tile, step):
            pixels = pixel_scratch[n, start : start + step].reshape(step * box, box)
            h = lax.dot_general(
                x_rows, pixels, (((1,), (1,)), ((), ())), preferred_element_type=jnp.float32
            )
            for i in range(step):
                at = (start + i) * ROW_PAD
                rows_scratch[at : at + ROW_PAD, :] = h[:, i * box : (i + 1) * box]
        for k in range(HALF + 1):
            for c in range(2):
                j = c * (HALF + 1) + k
                picked = rows_scratch[pl.ds(j, tile, stride=ROW_PAD), :]
                lhs_scratch[k * tile : (k + 1) * tile, c * box : (c + 1) * box] = picked.astype(jnp.bfloat16)
        here = pl.ds(pl.multiple_of(kept + n * tile, tile), tile)
        special = jnp.zeros((tile, LANES), jnp.float32)
        for k in range(HALF + 1):
            if k % batch == 0:
                many = jnp.dot(
                    lhs_scratch[k * tile : (k + batch) * tile, :], y_rows, preferred_element_type=jnp.float32
                )
            both = many[(k % batch) * tile : (k % batch + 1) * tile]
            value = both[:, :LANES]
            if k < HALF:
                out_ref[here, group(k)] = value.astype(jnp.bfloat16)
            else:
                special = jnp.where(q <= HALF, value, special)
            if 0 < k < HALF:
                special = jnp.where(q == KWIN - k, both[:, LANES:], special)
        out_ref[here, group(HALF)] = special.astype(jnp.bfloat16)
        return carry

    lax.fori_loop(0, tiles, one, 0)


def dft(images, table, tile, first, count, before=()):
    box = images.shape[1]
    total = count + sum(b.shape[0] for b in before)
    return pl.pallas_call(
        functools.partial(dft_kernel, tile, first),
        in_specs=[pl.BlockSpec(memory_space=pltpu.VMEM), pl.BlockSpec(memory_space=pl.ANY)]
        + [pl.BlockSpec(memory_space=pltpu.VMEM)] * len(before),
        out_shape=jax.ShapeDtypeStruct((total, UNIQUE), jnp.bfloat16),
        scratch_shapes=[
            pltpu.VMEM((count // tile, tile, box, box), jnp.bfloat16),
            pltpu.VMEM(((tile + 1) * ROW_PAD, box), jnp.float32),
            pltpu.VMEM(((HALF + 1) * tile, 2 * box), jnp.bfloat16),
            pltpu.SemaphoreType.DMA((count // tile,)),
        ],
        cost_estimate=pl.CostEstimate(
            flops=count * (2 * box * box * ROW_PAD + 2 * (HALF + 1) * 2 * box * LANES * 2),
            bytes_accessed=2 * count * (box * box + UNIQUE),
            transcendentals=0,
        ),
        compiler_params=params(46),
        name="dft",
    )(table, images, *before)


def stacked_rows(at, base_ref, rows, particles):
    parts = [
        lax.broadcasted_iota(jnp.int32, (rows, particles), 0) + base_ref[n] for n in at
    ]
    return jnp.concatenate(parts, axis=0) if len(parts) > 1 else parts[0]


def stacked_rows(at, base_ref, rows, particles):
    parts = [
        lax.broadcasted_iota(jnp.int32, (rows, particles), 0) + base_ref[n] for n in at
    ]
    return jnp.concatenate(parts, axis=0) if len(parts) > 1 else parts[0]


def score_kernel(items, halves, base_ref, panel_ref, before_ref, *rest):
    specs, refs, out_ref = rest[:halves], list(rest[halves:-1]), rest[-1]
    rows = refs[0].shape[0]
    taken = []
    for at, first, width in items:
        blocks = [refs.pop(0)[...] for _ in at]
        taken.append((at, first, width, jnp.concatenate(blocks, axis=0) if len(blocks) > 1 else blocks[0]))
    edge = 0
    for spec_ref in specs:
        particles = spec_ref.shape[0]
        lanes = slice(edge, edge + particles)
        edge += particles
        picked = [before_ref[t : t + 1, lanes] for t in range(TOP)]
        for at, first, width, block in taken:
            s = lax.dot_general(
                block,
                spec_ref[:, first : first + width],
                (((1,), (1,)), ((), ())),
                preferred_element_type=jnp.float32,
            )
            row = stacked_rows(at, base_ref, rows, particles)
            for t in range(TOP):
                hit = row == panel_ref[t : t + 1, lanes]
                picked[t] = picked[t] + jnp.sum(jnp.where(hit, s, 0.0), axis=0, keepdims=True)
        for t in range(TOP):
            out_ref[t : t + 1, lanes] = picked[t]


def score(bases, spectra, panel, before, items):
    rows = items[0][2][0].shape[0]
    refs = [r for _, _, blocks in items for r in blocks]
    values = sum(r.shape[1] for r in refs) * rows
    shapes = [(at, first, blocks[0].shape[1]) for at, first, blocks in items]
    return pl.pallas_call(
        functools.partial(score_kernel, shapes, len(spectra)),
        in_specs=[pl.BlockSpec(memory_space=pltpu.SMEM)]
        + [pl.BlockSpec(memory_space=pltpu.VMEM)] * (2 + len(spectra) + len(refs)),
        out_shape=jax.ShapeDtypeStruct(panel.shape, jnp.float32),
        cost_estimate=pl.CostEstimate(
            flops=2 * values * panel.shape[1], bytes_accessed=2 * values, transcendentals=0
        ),
        compiler_params=params(),
        name="score",
    )(bases, panel, before, *spectra, *refs)


def softmax(score_refs, prior_ref, precision_ref):
    total = score_refs[0][...]
    for ref in score_refs[1:]:
        total = total + ref[...]
    value = total * precision_ref[...]
    unscaled = prior_ref[...] * jnp.exp(value - jnp.max(value, axis=0, keepdims=True))
    weight = unscaled / jnp.sum(unscaled, axis=0, keepdims=True)
    return weight.astype(jnp.bfloat16).astype(jnp.float32)


def sums_kernel(items, halves, count, base_ref, panel_ref, *rest):
    specs, given, outs = rest[:halves], rest[halves : halves + count], list(rest[halves + count :])
    particles = panel_ref.shape[1]
    if count == 1:
        weight_ref = given[0]
    else:
        weight_ref = outs.pop(0)
        weight_ref[...] = softmax(given[:-2], *given[-2:])
    for at, first in items:
        rows, width = outs[0].shape
        row = stacked_rows(at, base_ref, rows, particles)
        select = jnp.zeros(row.shape, jnp.float32)
        for t in range(TOP):
            select = select + jnp.where(row == panel_ref[t : t + 1, :], weight_ref[t : t + 1, :], 0.0)
        select = select.astype(jnp.bfloat16)
        total, edge = None, 0
        for spec_ref in specs:
            count = spec_ref.shape[0]
            term = jnp.dot(
                select[:, edge : edge + count],
                spec_ref[:, first : first + width],
                preferred_element_type=jnp.float32,
            )
            total = term if total is None else total + term
            edge += count
        for n in range(len(at)):
            out_ref = outs.pop(0)
            out_ref[...] = total[n * rows : (n + 1) * rows].astype(out_ref.dtype)


def sums(bases, weight, panel, spectra, rows, items, dtype):
    particles = panel.shape[1]
    given = list(weight) if isinstance(weight, (list, tuple)) else [weight]
    shapes = [(rows, width) for at, _, width in items for _ in at]
    values = sum(a * b for a, b in shapes)
    out_shape = [jax.ShapeDtypeStruct(shape, dtype) for shape in shapes]
    if len(given) > 1:
        out_shape = [jax.ShapeDtypeStruct(panel.shape, jnp.float32)] + out_shape
    return pl.pallas_call(
        functools.partial(sums_kernel, [(at, first) for at, first, _ in items], len(spectra), len(given)),
        in_specs=[pl.BlockSpec(memory_space=pltpu.SMEM)]
        + [pl.BlockSpec(memory_space=pltpu.VMEM)] * (1 + len(spectra) + len(given)),
        out_shape=out_shape,
        cost_estimate=pl.CostEstimate(
            flops=2 * values * particles, bytes_accessed=4 * values, transcendentals=0
        ),
        compiler_params=params(),
        name="sums",
    )(bases, panel, *spectra, *given)


RING = (0, 2, 4, 6, 7, 5, 3, 1)


def ring_places():
    count = len(RING)
    table = np.zeros((count, count), np.int32)
    for at, place in enumerate(RING):
        table[place] = [RING[(at + d) % count] for d in range(count)]
    return table


def onward(value):
    return lax.ppermute(value, "dp", list(zip(RING, RING[1:] + RING[:1])))


def backward(value):
    return lax.ppermute(value, "dp", list(zip(RING[1:] + RING[:1], RING)))


def tie(*values):
    return lax.optimization_barrier(values)


def by_ring(images, references, panel, prior, precision):
    rows = references.shape[0]
    cls_count = lax.axis_size("cls")
    place, mine = lax.axis_index("dp"), lax.axis_index("cls")
    table = half_tables(images.shape[1])
    bases = (jnp.asarray(ring_places())[place] * cls_count + mine) * rows
    starts = (0, WIDTHS[0])

    own = fold(references)
    p1 = onward(own[0]), backward(own[1])
    q1 = onward(own[1]), backward(own[0])
    half = images.shape[0] // 2
    left = dft(images, table, 64, 0, half)
    *p1, left, table = tie(*p1, left, table)
    p2 = onward(p1[0]), backward(p1[1])
    *q1, table = tie(*q1, table)
    q2 = onward(q1[0]), backward(q1[1])
    right = dft(images, table, 64, half, half // 2)
    *p2, right, table = tie(*p2, right, table)
    p3 = onward(p2[0]), backward(p2[1])
    *q2, table = tie(*q2, table)
    q3 = onward(q2[0]), backward(q2[1])
    right = dft(images, table, 64, half + half // 2, half // 2, [right])
    spectra = [left, right]
    *p3, right = tie(*p3, right)
    spectra = [left, right]
    p4 = onward(p3[0]), backward(p3[1])
    picked = jnp.zeros(panel.shape, jnp.float32)
    near = [
        ((0, 7, 1), starts[0], [own[0], p1[0], q1[1]]),
        ((0, 7, 1), starts[1], [own[1], q1[0], p1[1]]),
        ((6, 2), starts[0], [p2[0], q2[1]]),
        ((6, 2), starts[1], [q2[0], p2[1]]),
    ]
    picked = score(bases, spectra, panel, picked, near)
    *q3, picked = tie(*q3, picked)
    middle = [((5, 3), starts[0], [p3[0], q3[1]]), ((5, 3), starts[1], [q3[0], p3[1]])]
    picked = score(bases, spectra, panel, picked, middle)
    for piece in range(2):
        arrived, picked = tie(p4[piece], picked)
        picked = score(bases, spectra, panel, picked, [((4,), starts[piece], [arrived])])

    turns = [[(c, c ^ n) for c in range(cls_count)] for n in range(cls_count - 1, 0, -1)]
    weight = [picked] + [lax.ppermute(picked, "cls", turn) for turn in turns] + [prior, precision]

    narrow, wide = jnp.bfloat16, jnp.float32
    pieces = [(starts[p], WIDTHS[p]) for p in range(2)]

    def part(places, dtype):
        items = [(at, *piece) for at, piece in zip(zip(*places), pieces)]
        return sums(bases, weight, panel, spectra, rows, items, dtype)

    def pass_on(arrived, held):
        onto = [(h + a.astype(wide)).astype(narrow) for h, a in zip(held, arrived)]
        return onward(onto[0]), backward(onto[1])

    weight, far0, back0, far1, ahead1 = part([(4, 4), (5, 3)], narrow)
    p = onward(far0), backward(far1)
    q = onward(ahead1), backward(back0)
    held = list(part([(3, 5)], wide))
    *p, weight, held[0], held[1] = tie(*p, weight, *held)
    p = pass_on(p, held)
    held = list(part([(6, 2)], wide))
    *q, weight, held[0], held[1] = tie(*q, weight, *held)
    q = pass_on(q, held[::-1])
    held = list(part([(2, 6)], wide))
    *p, weight, held[0], held[1] = tie(*p, weight, *held)
    p = pass_on(p, held)
    held = list(part([(7, 1)], wide))
    *q, weight, held[0], held[1] = tie(*q, weight, *held)
    q = pass_on(q, held[::-1])
    held = list(part([(1, 7)], wide))
    *p, weight, held[0], held[1] = tie(*p, weight, *held)
    p = pass_on(p, held)
    kept = part([(0, 0)], wide)
    return unfold([kept[0], p[0], q[1]], [kept[1], q[0], p[1]])


def by_collectives(images, references, panel, prior, precision):
    rows = references.shape[0]
    dp_count = lax.axis_size("dp")
    cls_count = lax.axis_size("cls")
    mine = lax.axis_index("cls")
    table = half_tables(images.shape[1])
    own = jnp.concatenate(fold(references), axis=1)
    gathered = lax.all_gather(own, "dp", axis=0, tiled=False)
    half = images.shape[0] // 2
    spectra = [dft(images, table, 64, part * half, half) for part in range(2)]
    bases = (jnp.arange(dp_count, dtype=jnp.int32) * cls_count + mine) * rows
    picked = jnp.zeros(panel.shape, jnp.float32)
    items = [((n,), 0, [gathered[n]]) for n in range(dp_count)]
    for start in range(0, dp_count, 8):
        picked = score(bases, spectra, panel, picked, items[start : start + 8])
    scores = lax.all_gather(picked, "cls", axis=0, tiled=False)
    weight = [scores[n] for n in range(cls_count)] + [prior, precision]
    partial = []
    for start in range(0, dp_count, 8):
        items = [((n,), 0, UNIQUE) for n in range(start, min(start + 8, dp_count))]
        made = sums(bases, weight, panel, spectra, rows, items, jnp.bfloat16)
        weight, made = (made[0], made[1:]) if start == 0 else (weight, made)
        partial += made
    half = lax.psum_scatter(jnp.stack(partial), "dp", scatter_dimension=0, tiled=False)
    return unfold([half[:, : WIDTHS[0]]], [half[:, WIDTHS[0] :]])


def on_device(images, references, best_class, best_rot, prior, precision):
    panel = (best_class * ROTS + best_rot).T
    plan = by_ring if lax.axis_size("dp") == len(RING) else by_collectives
    return plan(images, references, panel, prior.T, precision[None, :])


def solution(mesh):
    in_specs = (
        P("dp", None, None),
        P(("dp", "cls"), None),
        P("dp", None),
        P("dp", None),
        P("dp", None),
        P("dp"),
    )
    out_specs = P(("dp", "cls"), None)
    return jax.shard_map(on_device, mesh=mesh, in_specs=in_specs, out_specs=out_specs, check_vma=False)
```

```python
import functools
import math

import numpy as np
import jax
import jax.numpy as jnp
from jax import lax
from jax.experimental import pallas as pl
from jax.experimental.pallas import tpu as pltpu
from jax.sharding import PartitionSpec as P

KWIN = 64
HALF = KWIN // 2
ROTS = 36
TOP = 4
LANES = 2 * KWIN
UNIQUE = (HALF + 1) * LANES
ROW_PAD = 72
CUT = 17
WIDTHS = (CUT * LANES, UNIQUE - CUT * LANES)


def half_tables(box):
    positions = np.arange(box, dtype=np.float32)
    frequencies = np.arange(KWIN, dtype=np.float32) - float(HALF)
    phase_x = (2.0 * math.pi * positions[:, None] * frequencies[None, : HALF + 1] / box).astype(np.float32)
    x_rows = np.zeros((ROW_PAD, box), np.float32)
    x_rows[: HALF + 1] = np.cos(phase_x).T / box
    x_rows[HALF + 1 : 2 * HALF + 2] = -np.sin(phase_x).T / box
    angle = (2.0 * math.pi * positions[:, None] * frequencies[None, :] / box).astype(np.float32)
    cosine, sine = np.cos(angle), np.sin(angle)
    y_rows = np.zeros((2 * box, 2 * LANES), np.float32)
    y_rows[:box, :KWIN] = cosine
    y_rows[:box, KWIN:LANES] = -sine
    y_rows[box:, :KWIN] = sine
    y_rows[box:, KWIN:LANES] = cosine
    y_rows[:box, LANES : LANES + KWIN] = cosine[:, :1]
    y_rows[:box, LANES + KWIN :] = -sine[:, :1]
    y_rows[box:, LANES : LANES + KWIN] = -sine[:, :1]
    y_rows[box:, LANES + KWIN :] = -cosine[:, :1]
    x_wide = np.concatenate([x_rows, np.zeros((ROW_PAD, 2 * LANES - box), np.float32)], axis=1)
    return jnp.asarray(np.concatenate([y_rows, x_wide]), jnp.bfloat16)


def mirror_matrix():
    row = lax.broadcasted_iota(jnp.int32, (LANES, LANES), 0)
    col = lax.broadcasted_iota(jnp.int32, (LANES, LANES), 1)
    value = jnp.where(col < KWIN, 1.0, -1.0)
    hit = (row % KWIN + col % KWIN == KWIN) & (row // KWIN == col // KWIN)
    return jnp.where(hit, value, 0.0).astype(jnp.bfloat16)


def lane_q(shape):
    return lax.broadcasted_iota(jnp.int32, shape, 1) % KWIN


def full_spec(shape):
    return pl.BlockSpec(shape, lambda *_: (0,) * len(shape))


def params(megabytes=16):
    return pltpu.CompilerParams(vmem_limit_bytes=megabytes * 1024 * 1024)


def group(k):
    return slice(k * LANES, (k + 1) * LANES)


def fold_kernel(r_ref, *outs):
    rows = r_ref.shape[0]
    q = lane_q((rows, LANES))
    mirror = mirror_matrix()
    flip = lambda v: jnp.dot(v, mirror, preferred_element_type=jnp.float32)

    def put(k, value):
        out_ref, at = (outs[0], k) if k < CUT else (outs[1], k - CUT)
        out_ref[:, group(at)] = value.astype(out_ref.dtype)

    put(0, r_ref[:, group(0)])
    centre = r_ref[:, group(HALF)]
    special = centre.astype(jnp.float32)
    special = special + jnp.where((q >= 1) & (q < HALF), flip(centre), 0.0)
    for k in range(1, HALF):
        other = r_ref[:, group(KWIN - k)]
        put(k, r_ref[:, group(k)].astype(jnp.float32) + flip(other))
        edge = pltpu.roll(other.astype(jnp.float32), KWIN - k, 1)
        special = jnp.where(q == KWIN - k, edge, special)
    put(HALF, special)


def fold(references):
    rows = references.shape[0]
    return pl.pallas_call(
        fold_kernel,
        out_shape=[jax.ShapeDtypeStruct((rows, width), jnp.bfloat16) for width in WIDTHS],
        compiler_params=params(),
        name="fold",
    )(references)


def unfold_kernel(*rest):
    terms, (result_ref, out_ref, sems) = rest[:-3], rest[-3:]
    rows = out_ref.shape[0]
    q = lane_q((rows, LANES))
    mirror = mirror_matrix()
    count = len(terms) // 2
    chunk = 8
    width = chunk * LANES

    def copy(n):
        lanes = pl.ds(n * width, width)
        return pltpu.make_async_copy(out_ref.at[:, lanes], result_ref.at[:, lanes], sems.at[n])

    def total(k):
        chosen, at = (terms[:count], k) if k < CUT else (terms[count:], k - CUT)
        return sum(t[:, group(at)].astype(jnp.float32) for t in chosen)

    twice = jnp.concatenate([mirror, mirror], axis=0)

    def flip(v):
        high = v.astype(jnp.bfloat16)
        low = (v - high.astype(jnp.float32)).astype(jnp.bfloat16)
        return jnp.dot(
            jnp.concatenate([high, low], axis=1), twice, preferred_element_type=jnp.float32
        )

    special = total(HALF)
    out_ref[:, group(0)] = total(0)
    out_ref[:, group(HALF)] = jnp.where(q <= HALF, special, flip(special))
    for k in range(1, HALF):
        if k % chunk == 1:
            values = [total(n) for n in range(k, min(k + chunk, HALF))]
            flipped = flip(jnp.concatenate(values, axis=0))
        at = (k - 1) % chunk
        out_ref[:, group(k)] = values[at]
        edge = pltpu.roll(special, LANES - (KWIN - k), 1)
        out_ref[:, group(KWIN - k)] = jnp.where(q == 0, edge, flipped[at * rows : (at + 1) * rows])
        if (k + 1) % chunk == 0:
            copy(k // chunk).start()
        if k % chunk == 0:
            copy((KWIN - k) // chunk).start()
    copy(HALF // chunk).start()
    for n in range(KWIN // chunk):
        copy(n).wait()


def unfold(left, right):
    terms = list(left) + list(right)
    rows = terms[0].shape[0]
    return pl.pallas_call(
        unfold_kernel,
        in_specs=[pl.BlockSpec(memory_space=pltpu.VMEM)] * len(terms),
        out_specs=pl.BlockSpec(memory_space=pl.ANY),
        out_shape=jax.ShapeDtypeStruct((rows, KWIN * LANES), jnp.float32),
        scratch_shapes=[
            pltpu.VMEM((rows, KWIN * LANES), jnp.float32),
            pltpu.SemaphoreType.DMA((KWIN // 8,)),
        ],
        compiler_params=params(),
        name="unfold",
    )(*terms)


def dft_kernel(tile, first, table_ref, img_ref, *rest):
    out_ref, pixel_scratch, rows_scratch, lhs_scratch, sems = rest[-5:]
    tiles, box = pixel_scratch.shape[0], img_ref.shape[1]
    kept = out_ref.shape[0] - tiles * tile

    def copy(n):
        return pltpu.make_async_copy(
            img_ref.at[pl.ds(first + n * tile, tile)], pixel_scratch.at[n], sems.at[n]
        )

    for n in range(tiles):
        copy(n).start()
    if kept:
        out_ref[:kept] = rest[0][...]
    y_rows = table_ref[: 2 * box, :]
    x_rows = table_ref[2 * box :, :box]
    q = lane_q((tile, LANES))
    step, batch = 8, 11

    def one(n, carry):
        copy(n).wait()
        for start in range(0, tile, step):
            pixels = pixel_scratch[n, start : start + step].reshape(step * box, box)
            h = lax.dot_general(
                x_rows, pixels, (((1,), (1,)), ((), ())), preferred_element_type=jnp.float32
            )
            for i in range(step):
                at = (start + i) * ROW_PAD
                rows_scratch[at : at + ROW_PAD, :] = h[:, i * box : (i + 1) * box]
        for k in range(HALF + 1):
            for c in range(2):
                j = c * (HALF + 1) + k
                picked = rows_scratch[pl.ds(j, tile, stride=ROW_PAD), :]
                lhs_scratch[k * tile : (k + 1) * tile, c * box : (c + 1) * box] = picked.astype(jnp.bfloat16)
        here = pl.ds(pl.multiple_of(kept + n * tile, tile), tile)
        special = jnp.zeros((tile, LANES), jnp.float32)
        for k in range(HALF + 1):
            if k % batch == 0:
                many = jnp.dot(
                    lhs_scratch[k * tile : (k + batch) * tile, :], y_rows, preferred_element_type=jnp.float32
                )
            both = many[(k % batch) * tile : (k % batch + 1) * tile]
            value = both[:, :LANES]
            if k < HALF:
                out_ref[here, group(k)] = value.astype(jnp.bfloat16)
            else:
                special = jnp.where(q <= HALF, value, special)
            if 0 < k < HALF:
                special = jnp.where(q == KWIN - k, both[:, LANES:], special)
        out_ref[here, group(HALF)] = special.astype(jnp.bfloat16)
        return carry

    lax.fori_loop(0, tiles, one, 0)


def dft(images, table, tile, first, count, before=()):
    box = images.shape[1]
    total = count + sum(b.shape[0] for b in before)
    return pl.pallas_call(
        functools.partial(dft_kernel, tile, first),
        in_specs=[pl.BlockSpec(memory_space=pltpu.VMEM), pl.BlockSpec(memory_space=pl.ANY)]
        + [pl.BlockSpec(memory_space=pltpu.VMEM)] * len(before),
        out_shape=jax.ShapeDtypeStruct((total, UNIQUE), jnp.bfloat16),
        scratch_shapes=[
            pltpu.VMEM((count // tile, tile, box, box), jnp.bfloat16),
            pltpu.VMEM(((tile + 1) * ROW_PAD, box), jnp.float32),
            pltpu.VMEM(((HALF + 1) * tile, 2 * box), jnp.bfloat16),
            pltpu.SemaphoreType.DMA((count // tile,)),
        ],
        cost_estimate=pl.CostEstimate(
            flops=count * (2 * box * box * ROW_PAD + 2 * (HALF + 1) * 2 * box * LANES * 2),
            bytes_accessed=2 * count * (box * box + UNIQUE),
            transcendentals=0,
        ),
        compiler_params=params(46),
        name="dft",
    )(table, images, *before)


def stacked_rows(at, base_ref, rows, particles):
    parts = [
        lax.broadcasted_iota(jnp.int32, (rows, particles), 0) + base_ref[n] for n in at
    ]
    return jnp.concatenate(parts, axis=0) if len(parts) > 1 else parts[0]


def stacked_rows(at, base_ref, rows, particles):
    parts = [
        lax.broadcasted_iota(jnp.int32, (rows, particles), 0) + base_ref[n] for n in at
    ]
    return jnp.concatenate(parts, axis=0) if len(parts) > 1 else parts[0]


def score_kernel(items, halves, base_ref, panel_ref, before_ref, *rest):
    specs, refs, out_ref = rest[:halves], list(rest[halves:-1]), rest[-1]
    rows = refs[0].shape[0]
    taken = []
    for at, first, width in items:
        blocks = [refs.pop(0)[...] for _ in at]
        taken.append((at, first, width, jnp.concatenate(blocks, axis=0) if len(blocks) > 1 else blocks[0]))
    edge = 0
    for spec_ref in specs:
        particles = spec_ref.shape[0]
        lanes = slice(edge, edge + particles)
        edge += particles
        picked = [before_ref[t : t + 1, lanes] for t in range(TOP)]
        for at, first, width, block in taken:
            s = lax.dot_general(
                block,
                spec_ref[:, first : first + width],
                (((1,), (1,)), ((), ())),
                preferred_element_type=jnp.float32,
            )
            row = stacked_rows(at, base_ref, rows, particles)
            for t in range(TOP):
                hit = row == panel_ref[t : t + 1, lanes]
                picked[t] = picked[t] + jnp.sum(jnp.where(hit, s, 0.0), axis=0, keepdims=True)
        for t in range(TOP):
            out_ref[t : t + 1, lanes] = picked[t]


def score(bases, spectra, panel, before, items):
    rows = items[0][2][0].shape[0]
    refs = [r for _, _, blocks in items for r in blocks]
    values = sum(r.shape[1] for r in refs) * rows
    shapes = [(at, first, blocks[0].shape[1]) for at, first, blocks in items]
    return pl.pallas_call(
        functools.partial(score_kernel, shapes, len(spectra)),
        in_specs=[pl.BlockSpec(memory_space=pltpu.SMEM)]
        + [pl.BlockSpec(memory_space=pltpu.VMEM)] * (2 + len(spectra) + len(refs)),
        out_shape=jax.ShapeDtypeStruct(panel.shape, jnp.float32),
        cost_estimate=pl.CostEstimate(
            flops=2 * values * panel.shape[1], bytes_accessed=2 * values, transcendentals=0
        ),
        compiler_params=params(),
        name="score",
    )(bases, panel, before, *spectra, *refs)


def softmax(score_refs, prior_ref, precision_ref):
    total = score_refs[0][...]
    for ref in score_refs[1:]:
        total = total + ref[...]
    value = total * precision_ref[...]
    unscaled = prior_ref[...] * jnp.exp(value - jnp.max(value, axis=0, keepdims=True))
    weight = unscaled / jnp.sum(unscaled, axis=0, keepdims=True)
    return weight.astype(jnp.bfloat16).astype(jnp.float32)


def sums_kernel(items, halves, count, base_ref, panel_ref, *rest):
    specs, given, outs = rest[:halves], rest[halves : halves + count], list(rest[halves + count :])
    particles = panel_ref.shape[1]
    if count == 1:
        weight_ref = given[0]
    else:
        weight_ref = outs.pop(0)
        weight_ref[...] = softmax(given[:-2], *given[-2:])
    for at, first in items:
        rows, width = outs[0].shape
        row = stacked_rows(at, base_ref, rows, particles)
        select = jnp.zeros(row.shape, jnp.float32)
        for t in range(TOP):
            select = select + jnp.where(row == panel_ref[t : t + 1, :], weight_ref[t : t + 1, :], 0.0)
        select = select.astype(jnp.bfloat16)
        total, edge = None, 0
        for spec_ref in specs:
            count = spec_ref.shape[0]
            term = jnp.dot(
                select[:, edge : edge + count],
                spec_ref[:, first : first + width],
                preferred_element_type=jnp.float32,
            )
            total = term if total is None else total + term
            edge += count
        for n in range(len(at)):
            out_ref = outs.pop(0)
            out_ref[...] = total[n * rows : (n + 1) * rows].astype(out_ref.dtype)


def sums(bases, weight, panel, spectra, rows, items, dtype):
    particles = panel.shape[1]
    given = list(weight) if isinstance(weight, (list, tuple)) else [weight]
    shapes = [(rows, width) for at, _, width in items for _ in at]
    values = sum(a * b for a, b in shapes)
    out_shape = [jax.ShapeDtypeStruct(shape, dtype) for shape in shapes]
    if len(given) > 1:
        out_shape = [jax.ShapeDtypeStruct(panel.shape, jnp.float32)] + out_shape
    return pl.pallas_call(
        functools.partial(sums_kernel, [(at, first) for at, first, _ in items], len(spectra), len(given)),
        in_specs=[pl.BlockSpec(memory_space=pltpu.SMEM)]
        + [pl.BlockSpec(memory_space=pltpu.VMEM)] * (1 + len(spectra) + len(given)),
        out_shape=out_shape,
        cost_estimate=pl.CostEstimate(
            flops=2 * values * particles, bytes_accessed=4 * values, transcendentals=0
        ),
        compiler_params=params(),
        name="sums",
    )(bases, panel, *spectra, *given)


RING = (0, 2, 4, 6, 7, 5, 3, 1)


def ring_places():
    count = len(RING)
    table = np.zeros((count, count), np.int32)
    for at, place in enumerate(RING):
        table[place] = [RING[(at + d) % count] for d in range(count)]
    return table


def onward(value):
    return lax.ppermute(value, "dp", list(zip(RING, RING[1:] + RING[:1])))


def backward(value):
    return lax.ppermute(value, "dp", list(zip(RING[1:] + RING[:1], RING)))


def tie(*values):
    return lax.optimization_barrier(values)


def by_ring(images, references, panel, prior, precision):
    rows = references.shape[0]
    cls_count = lax.axis_size("cls")
    place, mine = lax.axis_index("dp"), lax.axis_index("cls")
    table = half_tables(images.shape[1])
    bases = (jnp.asarray(ring_places())[place] * cls_count + mine) * rows
    starts = (0, WIDTHS[0])

    own = fold(references)
    p1 = onward(own[0]), backward(own[1])
    q1 = onward(own[1]), backward(own[0])
    half = images.shape[0] // 2
    left = dft(images, table, 64, 0, half)
    *p1, left, table = tie(*p1, left, table)
    p2 = onward(p1[0]), backward(p1[1])
    *q1, table = tie(*q1, table)
    q2 = onward(q1[0]), backward(q1[1])
    right = dft(images, table, 64, half, half // 2)
    *p2, right, table = tie(*p2, right, table)
    p3 = onward(p2[0]), backward(p2[1])
    *q2, table = tie(*q2, table)
    q3 = onward(q2[0]), backward(q2[1])
    right = dft(images, table, 64, half + half // 2, half // 2, [right])
    spectra = [left, right]
    *p3, right = tie(*p3, right)
    spectra = [left, right]
    p4 = onward(p3[0]), backward(p3[1])
    picked = jnp.zeros(panel.shape, jnp.float32)
    near = [
        ((0, 7, 1), starts[0], [own[0], p1[0], q1[1]]),
        ((0, 7, 1), starts[1], [own[1], q1[0], p1[1]]),
        ((6, 2), starts[0], [p2[0], q2[1]]),
        ((6, 2), starts[1], [q2[0], p2[1]]),
    ]
    picked = score(bases, spectra, panel, picked, near)
    *q3, picked = tie(*q3, picked)
    middle = [((5, 3), starts[0], [p3[0], q3[1]]), ((5, 3), starts[1], [q3[0], p3[1]])]
    picked = score(bases, spectra, panel, picked, middle)
    for piece in range(2):
        arrived, picked = tie(p4[piece], picked)
        picked = score(bases, spectra, panel, picked, [((4,), starts[piece], [arrived])])

    turns = [[(c, c ^ n) for c in range(cls_count)] for n in (*range(2, cls_count), 1)]
    weight = [picked] + [lax.ppermute(picked, "cls", turn) for turn in turns] + [prior, precision]

    narrow, wide = jnp.bfloat16, jnp.float32
    pieces = [(starts[p], WIDTHS[p]) for p in range(2)]

    def part(places, dtype):
        items = [(at, *piece) for at, piece in zip(zip(*places), pieces)]
        return sums(bases, weight, panel, spectra, rows, items, dtype)

    def pass_on(arrived, held):
        onto = [(h + a.astype(wide)).astype(narrow) for h, a in zip(held, arrived)]
        return onward(onto[0]), backward(onto[1])

    weight, far0, back0, far1, ahead1 = part([(4, 4), (5, 3)], narrow)
    p = onward(far0), backward(far1)
    q = onward(ahead1), backward(back0)
    held = list(part([(3, 5)], wide))
    *p, weight, held[0], held[1] = tie(*p, weight, *held)
    p = pass_on(p, held)
    held = list(part([(6, 2)], wide))
    *q, weight, held[0], held[1] = tie(*q, weight, *held)
    q = pass_on(q, held[::-1])
    held = list(part([(2, 6)], wide))
    *p, weight, held[0], held[1] = tie(*p, weight, *held)
    p = pass_on(p, held)
    held = list(part([(7, 1)], wide))
    *q, weight, held[0], held[1] = tie(*q, weight, *held)
    q = pass_on(q, held[::-1])
    held = list(part([(1, 7)], wide))
    *p, weight, held[0], held[1] = tie(*p, weight, *held)
    p = pass_on(p, held)
    kept = part([(0, 0)], wide)
    return unfold([kept[0], p[0], q[1]], [kept[1], q[0], p[1]])


def by_collectives(images, references, panel, prior, precision):
    rows = references.shape[0]
    dp_count = lax.axis_size("dp")
    cls_count = lax.axis_size("cls")
    mine = lax.axis_index("cls")
    table = half_tables(images.shape[1])
    own = jnp.concatenate(fold(references), axis=1)
    gathered = lax.all_gather(own, "dp", axis=0, tiled=False)
    half = images.shape[0] // 2
    spectra = [dft(images, table, 64, part * half, half) for part in range(2)]
    bases = (jnp.arange(dp_count, dtype=jnp.int32) * cls_count + mine) * rows
    picked = jnp.zeros(panel.shape, jnp.float32)
    items = [((n,), 0, [gathered[n]]) for n in range(dp_count)]
    for start in range(0, dp_count, 8):
        picked = score(bases, spectra, panel, picked, items[start : start + 8])
    scores = lax.all_gather(picked, "cls", axis=0, tiled=False)
    weight = [scores[n] for n in range(cls_count)] + [prior, precision]
    partial = []
    for start in range(0, dp_count, 8):
        items = [((n,), 0, UNIQUE) for n in range(start, min(start + 8, dp_count))]
        made = sums(bases, weight, panel, spectra, rows, items, jnp.bfloat16)
        weight, made = (made[0], made[1:]) if start == 0 else (weight, made)
        partial += made
    half = lax.psum_scatter(jnp.stack(partial), "dp", scatter_dimension=0, tiled=False)
    return unfold([half[:, : WIDTHS[0]]], [half[:, WIDTHS[0] :]])


def on_device(images, references, best_class, best_rot, prior, precision):
    panel = (best_class * ROTS + best_rot).T
    plan = by_ring if lax.axis_size("dp") == len(RING) else by_collectives
    return plan(images, references, panel, prior.T, precision[None, :])


def solution(mesh):
    in_specs = (
        P("dp", None, None),
        P(("dp", "cls"), None),
        P("dp", None),
        P("dp", None),
        P("dp", None),
        P("dp"),
    )
    out_specs = P(("dp", "cls"), None)
    return jax.shard_map(on_device, mesh=mesh, in_specs=in_specs, out_specs=out_specs, check_vma=False)
```
